256 devices in a mesh: row: 8 (over z_lo, core), col: 32 (over z_hi, y, x).
Axes of the slice: x: 4, y: 4, z: 8 (z_hi: 2, z_lo: 4; z = z_hi * 4 + z_lo), core: 2. Of those that a mesh axis runs over, the one named last changes fastest.
Arguments:
- features: bfloat16 [65536, 512], P(('row', 'col')), may hold values from -6 to 6
- pre_act: bfloat16 [65536, 512], P(('row', 'col')), may hold values from -6 to 6
- out_grad: bfloat16 [65536, 512], P(('row', 'col')), may hold values from -6 to 6
- weight: bfloat16 [512, 512], replicated, may hold values from -0.25 to 0.25
- tile_rows: int32 [8, 32, 256], P('row', 'col'), may hold values from 0 to 63
- tile_cols: int32 [8, 32, 256], P('row', 'col'), may hold values from 0 to 15
- tile_vals: bfloat16 [8, 32, 256, 128, 128], P('row', 'col'), may hold values from -0.0625 to 0.0625
- tile_counts: int32 [8, 32], P('row', 'col'), may hold values from 32 to 256, as said below
Outputs:
- feat_grad: bfloat16 [65536, 512], P(('row', 'col'))
- weight_grad: float32 [512, 512], replicated
- bias_grad: float32 [512], replicated
The draws below stay inside these ranges and needn't reach their ends.
Inputs may be any that keep to these rules, and one draw needn't show every extreme that they name: `tile_counts`: each grid cell holds 256, 128, 64 or 32 live tiles; at least one cell holds 256.
All inputs are finite; a program needn't handle non-finite values.
Results may differ from the reference program's by a relative error of at most 0.0049.
Values may be sent and summed in bfloat16 or wider, within the bound.
A program may use at most 128 MiB of HBM per device.

```python
import math
import jax
import jax.numpy as jnp
from jax import lax

F = 512
BLOCK = 128
ROWS_DEV = 256
TILES_DEV = 256
NODES = 65536
N_ROW = 8
N_COL = 32


def draw_tile_counts(key, part):
    key = jax.random.fold_in(key, 11)
    shift_key, top_key = jax.random.split(key)
    shifts = jax.random.randint(shift_key, (N_ROW * N_COL,), 0, 4)
    counts = jnp.right_shift(jnp.full((N_ROW * N_COL,), TILES_DEV, jnp.int32), shifts.astype(jnp.int32))
    busiest = jax.random.randint(top_key, (), 0, N_ROW * N_COL)
    counts = counts.at[busiest].set(TILES_DEV)
    return counts.reshape(N_ROW, N_COL).astype(jnp.int32)


def plant(entries, stream_key, least, largest):
    index_at = [jax.random.randint(jax.random.fold_in(stream_key, axis), (), 0, length) for axis, length in enumerate(entries.shape)]
    main_axis = entries.shape.index(max(entries.shape))
    beside = index_at[:main_axis] + [(index_at[main_axis] + 1) % entries.shape[main_axis]] + index_at[main_axis + 1:]
    return entries.at[tuple(index_at)].set(least).at[tuple(beside)].set(largest)


def steps_of(stream_key, dims, cuts, least, top_value):
    loudness = 1.0
    for axis_at, shards_of in cuts:
        steps = jax.random.uniform(jax.random.fold_in(jax.random.fold_in(stream_key, 6), axis_at), (shards_of,), jnp.float32, least / len(cuts), top_value / len(cuts))
        loudness = loudness * jnp.repeat(jnp.exp(steps), dims[axis_at] // shards_of).reshape((-1,) + (1,) * (len(dims) - 1 - axis_at))
    return loudness


def bell_draw(key, extent, scale, limit, cuts=(), kind=jnp.bfloat16):
    drawn = jax.random.normal(key, extent, jnp.float32) * scale
    if len(cuts) > 0:
        drawn = steps_of(key, extent, cuts, -0.22, 0.18) * drawn
    return jnp.clip(drawn, min=-limit, max=limit).astype(kind)


def setup_inputs(seed: int = 0) -> dict:
    key_of = jax.random.split(jax.random.key(seed), 9)
    return {
        "features": bell_draw(key_of[0], (NODES, F), 1.0, 6.0, ((0, 256),)),
        "pre_act": bell_draw(key_of[1], (NODES, F), 1.0, 6.0, ((0, 256),)),
        "out_grad": bell_draw(key_of[2], (NODES, F), 1.0, 6.0, ((0, 256),)),
        "weight": bell_draw(key_of[3], (F, F), F ** -0.5, 0.25),
        "tile_rows": plant(jax.random.randint(key_of[4], (N_ROW, N_COL, TILES_DEV), 0, N_COL * ROWS_DEV // 128), jax.random.fold_in(key_of[4], 1), 0, (N_COL * ROWS_DEV // 128) - 1).astype(jnp.int32),
        "tile_cols": plant(jax.random.randint(key_of[5], (N_ROW, N_COL, TILES_DEV), 0, N_ROW * ROWS_DEV // 128), jax.random.fold_in(key_of[5], 1), 0, (N_ROW * ROWS_DEV // 128) - 1).astype(jnp.int32),
        "tile_vals": bell_draw(key_of[6], (N_ROW, N_COL, TILES_DEV, BLOCK, BLOCK), (8192 * TILES_DEV // ROWS_DEV) ** -0.5, 0.0625, ((0, 8), (1, 32))),
        "tile_counts": draw_tile_counts(jax.random.fold_in(key_of[8], 71), 0),
    }


def reference(features, pre_act, out_grad, weight, tile_rows, tile_cols, tile_vals, tile_counts):
    masked = jnp.where(pre_act > 0, out_grad, jnp.zeros_like(out_grad))
    panel_size = N_COL * ROWS_DEV
    col_blocks = N_ROW * ROWS_DEV // 128
    tile_group = math.gcd(TILES_DEV, 64)

    def one_device(totals, device_index):
        grid_row = device_index // N_COL
        grid_col = device_index % N_COL
        grad_panel = lax.dynamic_slice_in_dim(masked, (grid_row * panel_size).astype(jnp.int32), panel_size, 0)
        grad_blocks = grad_panel.reshape(-1, 128, F)
        block_rows = tile_rows[grid_row, grid_col]
        block_cols = tile_cols[grid_row, grid_col]
        values = tile_vals[grid_row, grid_col]
        live_count = tile_counts[grid_row, grid_col]

        def add_tiles(column_acc, group_index):
            first_tile = (group_index * tile_group).astype(jnp.int32)
            rows_now = lax.dynamic_slice_in_dim(block_rows, first_tile, tile_group, 0)
            cols_now = lax.dynamic_slice_in_dim(block_cols, first_tile, tile_group, 0)
            vals_now = lax.dynamic_slice_in_dim(values, first_tile, tile_group, 0)
            gathered = jnp.take(grad_blocks, rows_now, axis=0)
            products = jnp.einsum('kab,kaf->kbf', vals_now.astype(jnp.float32), gathered.astype(jnp.float32))
            active = first_tile + jnp.arange(tile_group, dtype=jnp.int32) < live_count
            products = jnp.where(active[:, None, None], products, jnp.zeros_like(products))
            column_acc = column_acc + jax.ops.segment_sum(products, cols_now, num_segments=col_blocks)
            return (column_acc, None)
        start_acc = jnp.zeros((col_blocks, 128, F), jnp.float32)
        partial_sum = lax.scan(add_tiles, start_acc, jnp.arange(TILES_DEV // tile_group, dtype=jnp.int32))[0]
        partial_sum = partial_sum.reshape(N_ROW, ROWS_DEV, F)
        totals = totals.at[:, grid_col].add(partial_sum)
        return (totals, None)
    start_totals = jnp.zeros((N_ROW, N_COL, ROWS_DEV, F), jnp.float32)
    totals = lax.scan(one_device, start_totals, jnp.arange(N_ROW * N_COL, dtype=jnp.int32))[0]
    summed = totals.reshape(NODES, F)
    feat_grad = jnp.dot(summed.astype(jnp.bfloat16), weight.T, preferred_element_type=jnp.float32).astype(jnp.bfloat16)
    norm_scale = 1.0 / math.sqrt(NODES)
    weight_grad = jnp.dot(features.astype(jnp.float32).T, summed, precision=lax.Precision.HIGHEST) * norm_scale
    bias_grad = lax.optimization_barrier(jnp.sum(masked.astype(jnp.float32), axis=0)) * norm_scale
    return (feat_grad, weight_grad, bias_grad)
```

```python
import functools
import math

import jax
import jax.numpy as jnp
from jax import lax
from jax.experimental import pallas as pl
from jax.experimental.pallas import tpu as pltpu
from jax.sharding import PartitionSpec as P

AG_CHUNKS = 2
CHUNKS = 4
BLOCK = 128
MESH = pl.DeviceIdType.MESH


def gather_body(
    pre, cot, panel, bias_out, own_blocks, ag_send, ag_recv, own_sem
):
    rows_dev, width = pre.shape
    chunk = width // AG_CHUNKS
    half_chunk = chunk // 2

    r = lax.axis_index("row")
    c = lax.axis_index("col")
    zl, core = r // 2, r % 2
    zh, m = c // 16, c % 16
    y, x = m // 4, m % 4
    w8 = zh * 4 + zl
    partner = (r + 1 - 2 * core, c)
    z_partner = (r, (1 - zh) * 16 + m)

    def plane_peer(d):
        return (r, zh * 16 + (m + d) % 16)

    def z_peer(d):
        q = (w8 + d) % 8
        return (2 * (q % 4) + core, (q // 4) * 16 + m)

    def neighbour(dim, d):
        if dim == 0:
            return (r, zh * 16 + y * 4 + (x + d) % 4)
        return (r, zh * 16 + ((y + d) % 4) * 4 + x)

    def remote(src, dst, send_sem, recv_sem, device):
        return pltpu.make_async_remote_copy(
            src_ref=src, dst_ref=dst, send_sem=send_sem, recv_sem=recv_sem,
            device_id=device, device_id_type=MESH,
        )

    def wait_recv(ref, send_sem, recv_sem):
        remote(ref, ref, send_sem, recv_sem, partner).wait_recv()

    def wait_send(ref, send_sem, recv_sem):
        remote(ref, ref, send_sem, recv_sem, partner).wait_send()

    barrier = pltpu.get_barrier_semaphore()
    for device in (
        z_partner, neighbour(0, 1), neighbour(0, -1), neighbour(1, 1), neighbour(1, -1)
    ):
        pl.semaphore_signal(barrier, inc=1, device_id=device, device_id_type=MESH)

    def block_of(plane, d1, d2, h):
        if h == 0:
            xx, yy = (x + d1) % 4, (y + d2) % 4
        else:
            xx, yy = (x + d2) % 4, (y + d1) % 4
        return 2 * (plane * 16 + yy * 4 + xx) + h

    def ag_copy(k, b, device, part=None, h=None):
        ref = panel.at[k, b]
        if part is not None:
            ref = panel.at[k, b, pl.ds(part * half_chunk, half_chunk)]
        src = ref if h is None else own_blocks.at[k, h]
        remote(src, ref, ag_send.at[k], ag_recv.at[k, b], device).start()

    def ag_wait(k, b):
        wait_recv(panel.at[k, b], ag_send.at[k], ag_recv.at[k, b])

    def first_dim(h):
        return 0 if h == 0 else 1

    def second_dim(h):
        return 1 if h == 0 else 0

    def s0(k, plane, mine):
        for dim in (first_dim, second_dim):
            for h in (0, 1):
                b = block_of(plane, 0, 0, h)
                for d in (1, -1):
                    ag_copy(k, b, neighbour(dim(h), d), None, h if mine else None)

    def s1(k, plane):
        for d in (-1, 1):
            for h in (0, 1):
                b = block_of(plane, d, 0, h)
                ag_wait(k, b)
                ag_copy(k, b, neighbour(first_dim(h), -d), 0 if d == -1 else 1)
                for e in (1, -1):
                    ag_copy(k, b, neighbour(second_dim(h), e))

    def s2(k, plane):
        for h in (0, 1):
            b = block_of(plane, 2, 0, h)
            ag_wait(k, b)
            for e in (1, -1):
                ag_copy(k, b, neighbour(second_dim(h), e))

    def s3(k, plane):
        for d1 in (0, -1, 1, 2):
            for d in (-1, 1):
                for h in (0, 1):
                    b = block_of(plane, d1, d, h)
                    ag_wait(k, b)
                    ag_copy(k, b, neighbour(second_dim(h), -d), 0 if d == -1 else 1)

    def s4(k, plane):
        for d1 in (0, -1, 1, 2):
            for h in (0, 1):
                ag_wait(k, block_of(plane, d1, 2, h))

    def z_go(k):
        for h in (0, 1):
            b = block_of(zh, 0, 0, h)
            ag_copy(k, b, z_partner, None, h)

    def z_come(k):
        for h in (0, 1):
            ag_wait(k, block_of(1 - zh, 0, 0, h))
        s0(k, 1 - zh, False)

    places = []

    def prepare(k):
        lanes = pl.ds(k * chunk, chunk)
        kept = jnp.where(
            pre[:, lanes].astype(jnp.float32) > 0, cot[:, lanes].astype(jnp.float32), 0.0
        )
        for h in (0, 1):
            part = kept[h * BLOCK:(h + 1) * BLOCK, :]
            own_blocks[k, h] = part.T.astype(jnp.bfloat16)
        place = pltpu.make_async_copy(
            own_blocks.at[k], panel.at[k, pl.ds(2 * c, 2)], own_sem.at[k]
        )
        place.start()
        places.append(place)
        return jnp.sum(kept, axis=0, keepdims=True)

    bias_rows = [prepare(0)]
    pl.semaphore_wait(barrier, 5)
    s0(0, zh, True)
    z_go(0)
    for k in range(1, AG_CHUNKS):
        bias_rows.append(prepare(k))
        s0(k, zh, True)
        z_go(k)
    bias_out[...] = jnp.concatenate(bias_rows, axis=1)
    for k in range(AG_CHUNKS):
        s1(k, zh)
        s2(k, zh)
        if k > 0:
            s3(k - 1, 1 - zh)
            s4(k - 1, zh)
            s4(k - 1, 1 - zh)
        z_come(k)
        s3(k, zh)
        s1(k, 1 - zh)
        s2(k, 1 - zh)
    k = AG_CHUNKS - 1
    s3(k, 1 - zh)
    s4(k, zh)
    s4(k, 1 - zh)
    for place in places:
        place.wait()
    for k in range(AG_CHUNKS):
        wait_send(panel.at[k, pl.ds(0, 62)], ag_send.at[k], ag_recv.at[k, 0])


def order_body(trow, tcol, count, meta_v):
    n_tiles = trow.shape[1]
    n_cols = 16
    lane = lax.broadcasted_iota(jnp.int32, (n_tiles, n_tiles), 1)
    sub = lax.broadcasted_iota(jnp.int32, (n_tiles, n_tiles), 0)
    live = count[0, 0]
    lane1 = lax.broadcasted_iota(jnp.int32, (1, n_tiles), 1)
    col_r = jnp.where(lane1 < live, tcol[...], 100)
    diag = lane == sub
    col_c = jnp.sum(jnp.where(diag, col_r, 0), axis=1, keepdims=True)
    row_c = jnp.sum(jnp.where(diag, trow[...], 0), axis=1, keepdims=True)
    rank_c = jnp.sum(
        jnp.where((col_r == col_c) & (lane < sub), 1, 0), axis=1, keepdims=True
    )
    lane_j = lax.broadcasted_iota(jnp.int32, (n_tiles, BLOCK), 1)
    n_r = jnp.sum(jnp.where(col_c == lane_j, 1, 0), axis=0, keepdims=True)
    lane_j1 = lax.broadcasted_iota(jnp.int32, (1, BLOCK), 1)
    pad_r = jnp.where(lane_j1 < n_cols, n_r + (n_r & 1), 0)
    base_c = jnp.sum(jnp.where(lane_j < col_c, pad_r, 0), axis=1, keepdims=True)
    pos_c = jnp.where(col_c < n_cols, base_c + rank_c, 100000)
    jj_lane = lax.broadcasted_iota(jnp.int32, (BLOCK, BLOCK), 1)
    jj_sub = lax.broadcasted_iota(jnp.int32, (BLOCK, BLOCK), 0)
    pad_c = jnp.sum(jnp.where(jj_lane == jj_sub, pad_r, 0), axis=1, keepdims=True)
    end_r = jnp.sum(jnp.where(jj_sub <= jj_lane, pad_c, 0), axis=0, keepdims=True)
    last_r = jnp.maximum(end_r // 2 - 1, 0)
    has_r = jnp.where(n_r > 0, 1, 0)
    meta_w = meta_v.shape[1]
    lane_p = lax.broadcasted_iota(jnp.int32, (n_tiles, meta_w), 1)
    sub_p = lax.broadcasted_iota(jnp.int32, (n_tiles, meta_w), 0)
    hit = lane_p == pos_c
    meta_v[...] = jnp.zeros(meta_v.shape, jnp.int32)
    meta_v[0:1, :] = n_tiles + jnp.sum(
        jnp.where(hit, sub_p - n_tiles, 0), axis=0, keepdims=True
    )
    meta_v[1:2, :] = jnp.sum(jnp.where(hit, row_c, 0), axis=0, keepdims=True)
    meta_v[2:3, :] = 1 - jnp.sum(jnp.where(hit & (rank_c == 0), 1, 0), axis=0, keepdims=True)
    meta_v[3:4, 0:BLOCK] = last_r
    meta_v[4:5, 0:BLOCK] = has_r
    meta_v[5:6, 0:BLOCK] = jnp.sum(pad_r, axis=1, keepdims=True) // 2 + 0 * lane_j1


def product_body(meta_s, panel, vals, own, send, slots):
    chunk = panel.shape[1]
    core = lax.axis_index("row") % 2
    pairs = meta_s[5, 0]

    def step(p, acc):
        lhs = jnp.concatenate(
            [panel[meta_s[1, 2 * p]], panel[meta_s[1, 2 * p + 1]]], axis=1
        )
        both = [
            vals[jnp.minimum(meta_s[0, 2 * p + i], vals.shape[0] - 1)] for i in (0, 1)
        ]
        alive = (meta_s[0, 2 * p + 1] < vals.shape[0]).astype(jnp.int32).astype(jnp.bfloat16)
        rhs = jnp.concatenate([both[0], both[1] * alive], axis=0)
        keep = meta_s[2, 2 * p].astype(jnp.float32)
        acc = acc * keep + jnp.dot(lhs, rhs, preferred_element_type=jnp.float32)
        slots[p] = acc
        return acc

    def several(g, acc):
        for i in range(8):
            acc = step(8 * g + i, acc)
        return acc

    lax.fori_loop(0, (pairs + 7) // 8, several, jnp.zeros((chunk, BLOCK), jnp.float32))

    def column(j):
        return slots[meta_s[3, j]] * meta_s[4, j].astype(jnp.float32)

    for q in range(4):
        for h in (0, 1):
            other = column(2 * (2 * q + 1 - core) + h).astype(jnp.bfloat16)
            mine = column(2 * (2 * q + core) + h)
            for i in range(own.shape[0]):
                part = slice(i * own.shape[3], (i + 1) * own.shape[3])
                send[i, q, h] = other[part]
                own[i, q, h] = mine[part]


def reduce_body(
    norm_scale,
    own, send1, feat, weight, bias_in,
    fg_out, wg_out, bias_out,
    feat_t, recv1, total_f, send2, recv2, fg_acc, ar, recv_p, xs, recv_xy, zbuf, gathered, bxy, bz, bp,
    rs_send1, rs_recv1, rs_send2, rs_recv2,
    p_send, p_recv, xy_send, xy_recv, zr_send, zr_recv, g_send, g_recv, gp_send, gp_recv,
    b_send, b_recv,
):
    rows_dev, width = feat.shape
    chunk = width // CHUNKS

    r = lax.axis_index("row")
    c = lax.axis_index("col")
    zl, core = r // 2, r % 2
    zh, m = c // 16, c % 16
    y, x = m // 4, m % 4
    w8 = zh * 4 + zl
    partner = (r + 1 - 2 * core, c)
    z_partner = (r, (1 - zh) * 16 + m)

    def plane_peer(d):
        return (r, zh * 16 + (m + d) % 16)

    def z_peer(d):
        q = (w8 + d) % 8
        return (2 * (q % 4) + core, (q // 4) * 16 + m)

    def neighbour(dim, d):
        if dim == 0:
            return (r, zh * 16 + y * 4 + (x + d) % 4)
        return (r, zh * 16 + ((y + d) % 4) * 4 + x)

    def remote(src, dst, send_sem, recv_sem, device):
        return pltpu.make_async_remote_copy(
            src_ref=src, dst_ref=dst, send_sem=send_sem, recv_sem=recv_sem,
            device_id=device, device_id_type=MESH,
        )

    def wait_recv(ref, send_sem, recv_sem):
        remote(ref, ref, send_sem, recv_sem, partner).wait_recv()

    def wait_send(ref, send_sem, recv_sem):
        remote(ref, ref, send_sem, recv_sem, partner).wait_send()

    barrier = pltpu.get_barrier_semaphore()

    def greet(device):
        pl.semaphore_signal(barrier, inc=1, device_id=device, device_id_type=MESH)

    greet(partner)

    def greet_plane(d, carry):
        greet(plane_peer(d))
        return carry

    def greet_z(d, carry):
        greet(z_peer(d))
        return carry

    lax.fori_loop(1, 16, greet_plane, 0)
    lax.fori_loop(1, 8, greet_z, 0)
    bias_local = bias_in[...]
    bxy[m] = jnp.zeros(bxy.shape[1:], jnp.float32)
    for q in range(width // BLOCK):
        bxy[m, pl.ds(q, 1)] = bias_local[:, q * BLOCK:(q + 1) * BLOCK]

    def bias_plane(d, carry):
        remote(bxy.at[m], bxy.at[m], b_send.at[0], b_recv.at[0], plane_peer(d)).start()
        return carry

    def bias_z(d, carry):
        remote(bz.at[w8], bz.at[w8], b_send.at[1], b_recv.at[1], z_peer(d)).start()
        return carry

    feat_t[...] = feat[...].astype(jnp.float32).T.astype(jnp.bfloat16)
    pl.semaphore_wait(barrier, 23)
    for k in range(CHUNKS):
        remote(send1.at[k], recv1.at[k], rs_send1.at[k], rs_recv1.at[k], partner).start()

    def rs1(k):
        wait_recv(recv1.at[k], rs_send1.at[k], rs_recv1.at[k])
        for q in range(4):
            for h in (0, 1):
                total = own[k, q, h] + recv1[k, q, h].astype(jnp.float32)
                total_f[k, q, h] = total
                send2[k, q, h] = total.astype(jnp.bfloat16)
        for d in (1, 2, 3):
            q = (zl + d) % 4
            remote(
                send2.at[k, q], recv2.at[k, d - 1], rs_send2.at[k], rs_recv2.at[k],
                (2 * q + core, c),
            ).start()

    def rs2(k):
        wait_recv(recv2.at[k], rs_send2.at[k], rs_recv2.at[k])
        wg = None
        fg_parts = []
        w_part = weight[:, pl.ds(k * chunk, chunk)]
        for h in (0, 1):
            total = total_f[k, zl, h]
            for d in range(3):
                total = total + recv2[k, d, h].astype(jnp.float32)
            high = total.astype(jnp.bfloat16)
            low = (total - high.astype(jnp.float32)).astype(jnp.bfloat16)
            f_part = feat_t[:, h * BLOCK:(h + 1) * BLOCK]
            contract = (((1,), (1,)), ((), ()))
            for piece in (high, low):
                term = lax.dot_general(
                    f_part, piece, contract, preferred_element_type=jnp.float32
                )
                wg = term if wg is None else wg + term
            fg_parts.append(high)
        ar[k] = wg.reshape(ar.shape[1:])
        remote(
            ar.at[k, 1 - core], recv_p.at[k], p_send.at[k], p_recv.at[k], partner
        ).start()
        fg = jnp.dot(
            w_part, jnp.concatenate(fg_parts, axis=1), preferred_element_type=jnp.float32
        )
        if k == 0:
            fg_acc[...] = fg
        elif k < CHUNKS - 1:
            fg_acc[...] += fg
        else:
            fg_out[...] = (fg_acc[...] + fg).T.astype(jnp.bfloat16)

    def ar1(k):
        wait_recv(recv_p.at[k], p_send.at[k], p_recv.at[k])
        xs[k] = ar[k, core] + recv_p[k]

        def go(d, carry):
            remote(
                xs.at[k, (m + d) % 16], recv_xy.at[k, d - 1],
                xy_send.at[k], xy_recv.at[k], plane_peer(d),
            ).start()
            return carry

        lax.fori_loop(1, 16, go, 0)

    def ar2(k):
        wait_recv(recv_xy.at[k], xy_send.at[k], xy_recv.at[k])
        zbuf[k, w8] = xs[k, m] + jnp.sum(recv_xy[k], axis=0)

        def go(d, carry):
            remote(
                zbuf.at[k, w8], zbuf.at[k, w8], zr_send.at[k], zr_recv.at[k], z_peer(d)
            ).start()
            return carry

        lax.fori_loop(1, 8, go, 0)

    def ar3(k):
        wait_recv(zbuf.at[k, pl.ds(0, 7)], zr_send.at[k], zr_recv.at[k])
        total = zbuf[k, 0]
        for i in range(1, 8):
            total = total + zbuf[k, i]
        gathered[k, core, m] = total * norm_scale

        def go(d, carry):
            ref = gathered.at[k, core, m]
            remote(ref, ref, g_send.at[k], g_recv.at[k], plane_peer(d)).start()
            return carry

        lax.fori_loop(1, 16, go, 0)

    def ar4(k):
        wait_recv(gathered.at[k, 0, pl.ds(0, 15)], g_send.at[k], g_recv.at[k])
        ref = gathered.at[k, core]
        remote(ref, ref, gp_send.at[k], gp_recv.at[k], partner).start()

    def ar5(k):
        wait_recv(gathered.at[k, 0], gp_send.at[k], gp_recv.at[k])
        wg_out[:, pl.ds(k * chunk, chunk)] = gathered[k].reshape(width, chunk)

    def bias1():
        wait_recv(bxy.at[pl.ds(0, 15)], b_send.at[0], b_recv.at[0])
        total = bxy[0]
        for i in range(1, 16):
            total = total + bxy[i]
        bz[w8] = total
        lax.fori_loop(1, 8, bias_z, 0)

    def bias2():
        wait_recv(bz.at[pl.ds(0, 7)], b_send.at[1], b_recv.at[1])
        total = bz[0]
        for i in range(1, 8):
            total = total + bz[i]
        bp[0] = total
        remote(bp.at[0], bp.at[1], b_send.at[2], b_recv.at[2], partner).start()

    def bias3():
        wait_recv(bp.at[1], b_send.at[2], b_recv.at[2])
        bias_out[...] = (bp[0] + bp[1]) * norm_scale

    for k in range(CHUNKS):
        rs1(k)
    lax.fori_loop(1, 16, bias_plane, 0)
    bias1()
    for k in range(CHUNKS):
        rs2(k)
        if k == 0:
            bias2()
        if k >= 1:
            ar2(k - 1)
        ar1(k)
        if k >= 1:
            ar3(k - 1)
        if k >= 2:
            ar4(k - 2)
        if k >= 3:
            ar5(k - 3)
    last = CHUNKS - 1
    bias3()
    ar2(last)
    ar4(last - 1)
    ar3(last)
    ar5(last - 2)
    ar5(last - 1)
    ar4(last)
    for k in range(CHUNKS):
        wait_send(send1.at[k], rs_send1.at[k], rs_recv1.at[k])
        wait_send(send2.at[k, pl.ds(0, 3)], rs_send2.at[k], rs_recv2.at[k])
        wait_send(ar.at[k, 0], p_send.at[k], p_recv.at[k])
        wait_send(xs.at[k, pl.ds(0, 15)], xy_send.at[k], xy_recv.at[k])
        wait_send(zbuf.at[k, pl.ds(0, 7)], zr_send.at[k], zr_recv.at[k])
        wait_send(gathered.at[k, 0, pl.ds(0, 15)], g_send.at[k], g_recv.at[k])
    wait_send(bxy.at[pl.ds(0, 15)], b_send.at[0], b_recv.at[0])
    wait_send(bz.at[pl.ds(0, 7)], b_send.at[1], b_recv.at[1])
    wait_send(bp.at[0], b_send.at[2], b_recv.at[2])
    ar5(last)
    for k in range(CHUNKS):
        wait_send(gathered.at[k, 0], gp_send.at[k], gp_recv.at[k])


def local(features, pre_act, out_grad, weight, tile_rows, tile_cols, tile_vals, tile_counts):
    rows_dev, width = features.shape
    slots = tile_rows.shape[2]
    chunk = width // CHUNKS
    ag_chunk = width // AG_CHUNKS
    n_pairs = (slots + 16) // 2 + 8
    pieces = width // 32
    vertices = rows_dev * lax.axis_size("row") * lax.axis_size("col")
    bf16, f32 = jnp.bfloat16, jnp.float32
    vmem = pl.BlockSpec(memory_space=pltpu.VMEM)
    smem = pl.BlockSpec(memory_space=pltpu.SMEM)
    anywhere = pl.BlockSpec(memory_space=pl.ANY)
    dma = pltpu.SemaphoreType.DMA
    limit = 56 * 1024 * 1024
    panel, bias_rows = pl.pallas_call(
        gather_body,
        out_shape=(
            jax.ShapeDtypeStruct((AG_CHUNKS, 64, ag_chunk, BLOCK), bf16),
            jax.ShapeDtypeStruct((1, width), f32),
        ),
        in_specs=[vmem, vmem],
        out_specs=(anywhere, vmem),
        scratch_shapes=[
            pltpu.VMEM((AG_CHUNKS, 2, ag_chunk, BLOCK), bf16),
            dma((AG_CHUNKS,)), dma((AG_CHUNKS, 64)), dma((AG_CHUNKS,)),
        ],
        compiler_params=pltpu.CompilerParams(
            collective_id=0, has_side_effects=True, vmem_limit_bytes=limit
        ),
    )(pre_act, out_grad)
    meta = pl.pallas_call(
        order_body,
        out_shape=jax.ShapeDtypeStruct((8, 384), jnp.int32),
        in_specs=[vmem, vmem, smem],
        out_specs=vmem,
    )(
        tile_rows.reshape(1, slots), tile_cols.reshape(1, slots), tile_counts.reshape(1, 1)
    )
    own, send = pl.pallas_call(
        product_body,
        out_shape=(
            jax.ShapeDtypeStruct((CHUNKS, 4, 2, chunk, BLOCK), f32),
            jax.ShapeDtypeStruct((CHUNKS, 4, 2, chunk, BLOCK), bf16),
        ),
        grid_spec=pltpu.PrefetchScalarGridSpec(
            num_scalar_prefetch=1,
            grid=(AG_CHUNKS,),
            in_specs=[
                pl.BlockSpec((None, 64, ag_chunk, BLOCK), lambda k, meta: (k, 0, 0, 0)),
                pl.BlockSpec((slots, BLOCK, BLOCK), lambda k, meta: (0, 0, 0)),
            ],
            out_specs=(
                pl.BlockSpec((CHUNKS // AG_CHUNKS, 4, 2, chunk, BLOCK), lambda k, meta: (k, 0, 0, 0, 0)),
                pl.BlockSpec((CHUNKS // AG_CHUNKS, 4, 2, chunk, BLOCK), lambda k, meta: (k, 0, 0, 0, 0)),
            ),
            scratch_shapes=[pltpu.VMEM((n_pairs, ag_chunk, BLOCK), f32)],
        ),
        compiler_params=pltpu.CompilerParams(vmem_limit_bytes=limit),
    )(meta, panel, tile_vals.reshape(slots, BLOCK, BLOCK))

    fg, wg, bias = pl.pallas_call(
        functools.partial(reduce_body, 1.0 / math.sqrt(vertices)),
        out_shape=(
            jax.ShapeDtypeStruct((rows_dev, width), bf16),
            jax.ShapeDtypeStruct((width, width), f32),
            jax.ShapeDtypeStruct((8, BLOCK), f32),
        ),
        in_specs=[vmem] * 5,
        out_specs=(vmem, vmem, vmem),
        scratch_shapes=[
            pltpu.VMEM((width, rows_dev), bf16),
            pltpu.VMEM((CHUNKS, 4, 2, chunk, BLOCK), bf16),
            pltpu.VMEM((CHUNKS, 4, 2, chunk, BLOCK), f32),
            pltpu.VMEM((CHUNKS, 4, 2, chunk, BLOCK), bf16),
            pltpu.VMEM((CHUNKS, 3, 2, chunk, BLOCK), bf16),
            pltpu.VMEM((width, rows_dev), f32),
            pltpu.VMEM((CHUNKS, 2, 16, pieces, chunk), f32),
            pltpu.VMEM((CHUNKS, 16, pieces, chunk), f32),
            pltpu.VMEM((CHUNKS, 16, pieces, chunk), f32),
            pltpu.VMEM((CHUNKS, 15, pieces, chunk), f32),
            pltpu.VMEM((CHUNKS, 8, pieces, chunk), f32),
            pltpu.VMEM((CHUNKS, 2, 16, pieces, chunk), f32),
            pltpu.VMEM((16, 8, BLOCK), f32),
            pltpu.VMEM((8, 8, BLOCK), f32),
            pltpu.VMEM((2, 8, BLOCK), f32),
        ] + [dma((CHUNKS,))] * 14 + [dma((3,))] * 2,
        compiler_params=pltpu.CompilerParams(
            collective_id=1, has_side_effects=True, vmem_limit_bytes=limit
        ),
    )(own, send, features, weight, bias_rows)
    return fg, wg, bias.reshape(-1)[:width]


def solution(mesh):
    placed = (
        P(("row", "col"), None),
        P(("row", "col"), None),
        P(("row", "col"), None),
        P(),
        P("row", "col", None),
        P("row", "col", None),
        P("row", "col", None, None, None),
        P("row", "col"),
    )
    return jax.shard_map(
        local,
        mesh=mesh,
        in_specs=placed,
        out_specs=(P(("row", "col"), None), P(), P()),
        check_vma=False,
    )
```

```python
import functools
import math

import jax
import jax.numpy as jnp
from jax import lax
from jax.experimental import pallas as pl
from jax.experimental.pallas import tpu as pltpu
from jax.sharding import PartitionSpec as P

AG_CHUNKS = 2
BLOCK = 128
MESH = pl.DeviceIdType.MESH


def gather_body(
    pre, cot, feat, trow, tcol, count, panel, feat_all, bias_out, meta_v,
    own_blocks, own_feat, ag_send, ag_recv, own_sem, f_send, f_recv
):
    rows_dev, width = pre.shape
    chunk = width // AG_CHUNKS
    half_chunk = chunk // 2

    r = lax.axis_index("row")
    c = lax.axis_index("col")
    zl, core = r // 2, r % 2
    zh, m = c // 16, c % 16
    y, x = m // 4, m % 4
    w8 = zh * 4 + zl
    partner = (r + 1 - 2 * core, c)
    z_partner = (r, (1 - zh) * 16 + m)

    def plane_peer(d):
        return (r, zh * 16 + (m + d) % 16)

    def z_peer(d):
        q = (w8 + d) % 8
        return (2 * (q % 4) + core, (q // 4) * 16 + m)

    def z_near(d):
        return (2 * ((zl + d) % 4) + core, c)

    def neighbour(dim, d):
        if dim == 0:
            return (r, zh * 16 + y * 4 + (x + d) % 4)
        return (r, zh * 16 + ((y + d) % 4) * 4 + x)

    def remote(src, dst, send_sem, recv_sem, device):
        return pltpu.make_async_remote_copy(
            src_ref=src, dst_ref=dst, send_sem=send_sem, recv_sem=recv_sem,
            device_id=device, device_id_type=MESH,
        )

    def wait_recv(ref, send_sem, recv_sem):
        remote(ref, ref, send_sem, recv_sem, partner).wait_recv()

    def wait_send(ref, send_sem, recv_sem):
        remote(ref, ref, send_sem, recv_sem, partner).wait_send()

    barrier = pltpu.get_barrier_semaphore()
    for device in (
        z_partner, neighbour(0, 1), neighbour(0, -1), neighbour(1, 1), neighbour(1, -1),
        z_near(1), z_near(2), z_near(3),
    ):
        pl.semaphore_signal(barrier, inc=1, device_id=device, device_id_type=MESH)

    def block_of(plane, d1, d2, h):
        if h == 0:
            xx, yy = (x + d1) % 4, (y + d2) % 4
        else:
            xx, yy = (x + d2) % 4, (y + d1) % 4
        return 2 * (plane * 16 + yy * 4 + xx) + h

    def ag_copy(k, b, device, part=None, h=None):
        ref = panel.at[k, b]
        if part is not None:
            ref = panel.at[k, b, pl.ds(part * half_chunk, half_chunk)]
        src = ref if h is None else own_blocks.at[k, h]
        remote(src, ref, ag_send.at[k], ag_recv.at[k, b], device).start()

    def ag_wait(k, b):
        wait_recv(panel.at[k, b], ag_send.at[k], ag_recv.at[k, b])

    def first_dim(h):
        return 0 if h == 0 else 1

    def second_dim(h):
        return 1 if h == 0 else 0

    def s0(k, plane, mine):
        for dim in (first_dim, second_dim):
            for h in (0, 1):
                b = block_of(plane, 0, 0, h)
                for d in (1, -1):
                    ag_copy(k, b, neighbour(dim(h), d), None, h if mine else None)

    def s1(k, plane):
        for d in (-1, 1):
            for h in (0, 1):
                b = block_of(plane, d, 0, h)
                ag_wait(k, b)
                ag_copy(k, b, neighbour(first_dim(h), -d), 0 if d == -1 else 1)
                for e in (1, -1):
                    ag_copy(k, b, neighbour(second_dim(h), e))

    def s2(k, plane):
        for h in (0, 1):
            b = block_of(plane, 2, 0, h)
            ag_wait(k, b)
            for e in (1, -1):
                ag_copy(k, b, neighbour(second_dim(h), e))

    def s3(k, plane):
        for d1 in (0, -1, 1, 2):
            for d in (-1, 1):
                for h in (0, 1):
                    b = block_of(plane, d1, d, h)
                    ag_wait(k, b)
                    ag_copy(k, b, neighbour(second_dim(h), -d), 0 if d == -1 else 1)

    def s4(k, plane):
        for d1 in (0, -1, 1, 2):
            for h in (0, 1):
                ag_wait(k, block_of(plane, d1, 2, h))

    def z_go(k):
        for h in (0, 1):
            b = block_of(zh, 0, 0, h)
            ag_copy(k, b, z_partner, None, h)

    def z_come(k):
        for h in (0, 1):
            ag_wait(k, block_of(1 - zh, 0, 0, h))
        s0(k, 1 - zh, False)

    places = []

    def prepare(k):
        lanes = pl.ds(k * chunk, chunk)
        kept = jnp.where(
            pre[:, lanes].astype(jnp.float32) > 0, cot[:, lanes].astype(jnp.float32), 0.0
        )
        for h in (0, 1):
            part = kept[h * BLOCK:(h + 1) * BLOCK, :]
            own_blocks[k, h] = part.T.astype(jnp.bfloat16)
        place = pltpu.make_async_copy(
            own_blocks.at[k], panel.at[k, pl.ds(2 * c, 2)], own_sem.at[k]
        )
        place.start()
        places.append(place)
        return jnp.sum(kept, axis=0, keepdims=True)

    def order_tiles():
        n_tiles = trow.shape[1]
        n_cols = 16
        lane = lax.broadcasted_iota(jnp.int32, (n_tiles, n_tiles), 1)
        sub = lax.broadcasted_iota(jnp.int32, (n_tiles, n_tiles), 0)
        live = count[0, 0]
        lane1 = lax.broadcasted_iota(jnp.int32, (1, n_tiles), 1)
        col_r = jnp.where(lane1 < live, tcol[...], 100)
        diag = lane == sub
        col_c = jnp.sum(jnp.where(diag, col_r, 0), axis=1, keepdims=True)
        row_c = jnp.sum(jnp.where(diag, trow[...], 0), axis=1, keepdims=True)
        rank_c = jnp.sum(
            jnp.where((col_r == col_c) & (lane < sub), 1, 0), axis=1, keepdims=True
        )
        lane_j = lax.broadcasted_iota(jnp.int32, (n_tiles, BLOCK), 1)
        n_r = jnp.sum(jnp.where(col_c == lane_j, 1, 0), axis=0, keepdims=True)
        lane_j1 = lax.broadcasted_iota(jnp.int32, (1, BLOCK), 1)
        pad_r = jnp.where(lane_j1 < n_cols, n_r + (n_r & 1), 0)
        base_c = jnp.sum(jnp.where(lane_j < col_c, pad_r, 0), axis=1, keepdims=True)
        pos_c = jnp.where(col_c < n_cols, base_c + rank_c, 100000)
        jj_lane = lax.broadcasted_iota(jnp.int32, (BLOCK, BLOCK), 1)
        jj_sub = lax.broadcasted_iota(jnp.int32, (BLOCK, BLOCK), 0)
        pad_c = jnp.sum(jnp.where(jj_lane == jj_sub, pad_r, 0), axis=1, keepdims=True)
        end_r = jnp.sum(jnp.where(jj_sub <= jj_lane, pad_c, 0), axis=0, keepdims=True)
        last_r = jnp.maximum(end_r // 2 - 1, 0)
        has_r = jnp.where(n_r > 0, 1, 0)
        meta_w = meta_v.shape[1]
        lane_p = lax.broadcasted_iota(jnp.int32, (n_tiles, meta_w), 1)
        sub_p = lax.broadcasted_iota(jnp.int32, (n_tiles, meta_w), 0)
        hit = lane_p == pos_c
        meta_v[...] = jnp.zeros(meta_v.shape, jnp.int32)
        meta_v[0:1, :] = n_tiles + jnp.sum(
            jnp.where(hit, sub_p - n_tiles, 0), axis=0, keepdims=True
        )
        meta_v[1:2, :] = jnp.sum(jnp.where(hit, row_c, 0), axis=0, keepdims=True)
        meta_v[2:3, :] = 1 - jnp.sum(jnp.where(hit & (rank_c == 0), 1, 0), axis=0, keepdims=True)
        meta_v[3:4, 0:BLOCK] = last_r
        meta_v[4:5, 0:BLOCK] = has_r
        meta_v[5:6, 0:BLOCK] = jnp.sum(pad_r, axis=1, keepdims=True) // 2 + 0 * lane_j1

    bias_rows = [prepare(0)]
    pl.semaphore_wait(barrier, 8)
    s0(0, zh, True)
    z_go(0)
    for k in range(1, AG_CHUNKS):
        bias_rows.append(prepare(k))
        s0(k, zh, True)
        z_go(k)
    bias_out[...] = jnp.concatenate(bias_rows, axis=1)
    own_feat[...] = feat[...].astype(jnp.float32).T.astype(jnp.bfloat16)
    for d in (1, 2, 3):
        remote(own_feat, feat_all.at[zl], f_send.at[0], f_recv.at[0], z_near(d)).start()
    place = pltpu.make_async_copy(own_feat, feat_all.at[zl], f_send.at[1])
    place.start()
    places.append(place)
    order_tiles()
    for k in range(AG_CHUNKS):
        s1(k, zh)
        s2(k, zh)
        if k > 0:
            s3(k - 1, 1 - zh)
            s4(k - 1, zh)
            s4(k - 1, 1 - zh)
        z_come(k)
        s3(k, zh)
        s1(k, 1 - zh)
        s2(k, 1 - zh)
    k = AG_CHUNKS - 1
    s3(k, 1 - zh)
    s4(k, zh)
    s4(k, 1 - zh)
    for place in places:
        place.wait()
    for k in range(AG_CHUNKS):
        wait_send(panel.at[k, pl.ds(0, 62)], ag_send.at[k], ag_recv.at[k, 0])
    wait_recv(feat_all.at[pl.ds(0, 3)], f_send.at[0], f_recv.at[0])
    wait_send(feat_all.at[pl.ds(0, 3)], f_send.at[0], f_recv.at[0])


def product_body(meta_s, panel, vals, own, send, slots):
    chunk = panel.shape[1]
    core = lax.axis_index("row") % 2
    pairs = meta_s[5, 0]

    def step(p, acc):
        lhs = jnp.concatenate(
            [panel[meta_s[1, 2 * p]], panel[meta_s[1, 2 * p + 1]]], axis=1
        )
        both = [
            vals[jnp.minimum(meta_s[0, 2 * p + i], vals.shape[0] - 1)] for i in (0, 1)
        ]
        alive = (meta_s[0, 2 * p + 1] < vals.shape[0]).astype(jnp.int32).astype(jnp.bfloat16)
        rhs = jnp.concatenate([both[0], both[1] * alive], axis=0)
        keep = meta_s[2, 2 * p].astype(jnp.float32)
        acc = acc * keep + jnp.dot(lhs, rhs, preferred_element_type=jnp.float32)
        slots[p] = acc
        return acc

    def several(g, acc):
        for i in range(8):
            acc = step(8 * g + i, acc)
        return acc

    lax.fori_loop(0, (pairs + 7) // 8, several, jnp.zeros((chunk, BLOCK), jnp.float32))

    def column(j):
        return slots[meta_s[3, j]] * meta_s[4, j].astype(jnp.float32)

    for q in range(4):
        for h in (0, 1):
            lanes = slice(h * BLOCK, (h + 1) * BLOCK)
            send[q, :, lanes] = column(2 * (2 * q + 1 - core) + h).astype(jnp.bfloat16)
            own[q, :, lanes] = column(2 * (2 * q + core) + h)


def reduce_body(
    norm_scale,
    own, send1, feat_all, weight, bias_in,
    fg_out, gathered, bias_out,
    recv1, total, send2, recv2, ar, recv_p, xs, recv_xy, zbuf, bxy, bz, bp,
    rs_send1, rs_recv1, rs_send2, rs_recv2, small_send, small_recv, b_send, b_recv,
):
    width = feat_all.shape[1]
    half = width // 2

    r = lax.axis_index("row")
    c = lax.axis_index("col")
    zl, core = r // 2, r % 2
    zh, m = c // 16, c % 16
    y, x = m // 4, m % 4
    w8 = zh * 4 + zl
    partner = (r + 1 - 2 * core, c)
    z_partner = (r, (1 - zh) * 16 + m)

    def plane_peer(d):
        return (r, zh * 16 + (m + d) % 16)

    def z_peer(d):
        q = (w8 + d) % 8
        return (2 * (q % 4) + core, (q // 4) * 16 + m)

    def z_near(d):
        return (2 * ((zl + d) % 4) + core, c)

    def neighbour(dim, d):
        if dim == 0:
            return (r, zh * 16 + y * 4 + (x + d) % 4)
        return (r, zh * 16 + ((y + d) % 4) * 4 + x)

    def remote(src, dst, send_sem, recv_sem, device):
        return pltpu.make_async_remote_copy(
            src_ref=src, dst_ref=dst, send_sem=send_sem, recv_sem=recv_sem,
            device_id=device, device_id_type=MESH,
        )

    def wait_recv(ref, send_sem, recv_sem):
        remote(ref, ref, send_sem, recv_sem, partner).wait_recv()

    def wait_send(ref, send_sem, recv_sem):
        remote(ref, ref, send_sem, recv_sem, partner).wait_send()

    barrier = pltpu.get_barrier_semaphore()

    def greet(device):
        pl.semaphore_signal(barrier, inc=1, device_id=device, device_id_type=MESH)

    greet(partner)

    def greet_plane(d, carry):
        greet(plane_peer(d))
        return carry

    def greet_z(d, carry):
        greet(z_peer(d))
        return carry

    lax.fori_loop(1, 16, greet_plane, 0)
    lax.fori_loop(1, 8, greet_z, 0)
    bias_local = bias_in[...]
    bxy[m] = jnp.zeros(bxy.shape[1:], jnp.float32)
    for q in range(width // BLOCK):
        bxy[m, pl.ds(q, 1)] = bias_local[:, q * BLOCK:(q + 1) * BLOCK]

    def bias_plane(d, carry):
        remote(bxy.at[m], bxy.at[m], b_send.at[0], b_recv.at[0], plane_peer(d)).start()
        return carry

    def bias_z(d, carry):
        remote(bz.at[w8], bz.at[w8], b_send.at[1], b_recv.at[1], z_peer(d)).start()
        return carry

    pl.semaphore_wait(barrier, 23)

    order = [(zl + d) % 4 for d in (1, 2, 3, 0)]
    for q in order:
        remote(
            send1.at[q], recv1.at[q], rs_send1.at[q], rs_recv1.at[q], partner
        ).start()
    lax.fori_loop(1, 16, bias_plane, 0)
    for i, q in enumerate(order):
        wait_recv(recv1.at[q], rs_send1.at[q], rs_recv1.at[q])
        pair = own[q] + recv1[q].astype(jnp.float32)
        send2[q] = pair.astype(jnp.bfloat16)
        if i < 3:
            remote(
                send2.at[q], recv2.at[i], rs_send2.at[i], rs_recv2.at[i], z_near(i + 1)
            ).start()
        else:
            total[...] = pair

    def term(which):
        rows = pl.ds(which * half, half)
        acc = None
        for q in order:
            piece = lax.dot_general(
                feat_all[q, rows, :], send2[q], (((1,), (1,)), ((), ())),
                preferred_element_type=jnp.float32,
            )
            acc = piece if acc is None else acc + piece
        return acc.reshape(recv_p.shape)

    ar[...] = term(1 - core)
    remote(ar, recv_p, small_send.at[0], small_recv.at[0], partner).start()
    mine = term(core)
    wait_recv(recv_p, small_send.at[0], small_recv.at[0])
    xs[...] = mine + recv_p[...]

    def go_xy(d, carry):
        remote(
            xs.at[(m + d) % 16], recv_xy.at[d - 1],
            small_send.at[1], small_recv.at[1], plane_peer(d),
        ).start()
        return carry

    lax.fori_loop(1, 16, go_xy, 0)

    wait_recv(bxy.at[pl.ds(0, 15)], b_send.at[0], b_recv.at[0])
    plane_sum = bxy[0]
    for i in range(1, 16):
        plane_sum = plane_sum + bxy[i]
    bz[w8] = plane_sum
    lax.fori_loop(1, 8, bias_z, 0)

    wait_recv(recv_xy, small_send.at[1], small_recv.at[1])
    zbuf[w8] = (xs[m] + jnp.sum(recv_xy[...], axis=0)).astype(zbuf.dtype)

    def go_z(d, carry):
        remote(
            zbuf.at[w8], zbuf.at[w8], small_send.at[2], small_recv.at[2], z_peer(d)
        ).start()
        return carry

    lax.fori_loop(1, 8, go_z, 0)

    wait_recv(bz.at[pl.ds(0, 7)], b_send.at[1], b_recv.at[1])
    z_sum = bz[0]
    for i in range(1, 8):
        z_sum = z_sum + bz[i]
    bp[0] = z_sum
    remote(bp.at[0], bp.at[1], b_send.at[2], b_recv.at[2], partner).start()

    wait_recv(zbuf.at[pl.ds(0, 7)], small_send.at[2], small_recv.at[2])
    grad = zbuf[0].astype(jnp.float32)
    for i in range(1, 8):
        grad = grad + zbuf[i].astype(jnp.float32)
    gathered[core, m] = grad * norm_scale

    def go_g(d, carry):
        ref = gathered.at[core, m]
        remote(ref, ref, small_send.at[3], small_recv.at[3], plane_peer(d)).start()
        return carry

    lax.fori_loop(1, 16, go_g, 0)

    summed = total[...]
    for d in range(3):
        wait_recv(recv2.at[d], rs_send2.at[d], rs_recv2.at[d])
        summed = summed + recv2[d].astype(jnp.float32)
    fg_out[...] = jnp.dot(
        weight[...], summed.astype(jnp.bfloat16), preferred_element_type=jnp.float32
    ).T.astype(jnp.bfloat16)
    wait_recv(bp.at[1], b_send.at[2], b_recv.at[2])
    bias_out[...] = (bp[0] + bp[1]) * norm_scale

    wait_recv(gathered.at[0, pl.ds(0, 15)], small_send.at[3], small_recv.at[3])
    ref = gathered.at[core]
    remote(ref, ref, small_send.at[4], small_recv.at[4], partner).start()
    for q in range(4):
        wait_send(send1.at[q], rs_send1.at[q], rs_recv1.at[q])
    for d in range(3):
        wait_send(recv2.at[d], rs_send2.at[d], rs_recv2.at[d])
    wait_send(ar, small_send.at[0], small_recv.at[0])
    wait_send(recv_xy, small_send.at[1], small_recv.at[1])
    wait_send(zbuf.at[pl.ds(0, 7)], small_send.at[2], small_recv.at[2])
    wait_send(gathered.at[0, pl.ds(0, 15)], small_send.at[3], small_recv.at[3])
    wait_send(bxy.at[pl.ds(0, 15)], b_send.at[0], b_recv.at[0])
    wait_send(bz.at[pl.ds(0, 7)], b_send.at[1], b_recv.at[1])
    wait_send(bp.at[0], b_send.at[2], b_recv.at[2])
    wait_recv(gathered.at[0], small_send.at[4], small_recv.at[4])
    wait_send(gathered.at[0], small_send.at[4], small_recv.at[4])


def finish_body(fg, wg, bias, fg_out, wg_out, bias_out):
    fg_out[...] = fg[...]
    wg_out[...] = wg[...]
    for q in range(bias_out.shape[0] // BLOCK):
        bias_out[pl.ds(q * BLOCK, BLOCK)] = bias[q]


def local(features, pre_act, out_grad, weight, tile_rows, tile_cols, tile_vals, tile_counts):
    rows_dev, width = features.shape
    slots = tile_rows.shape[2]
    ag_chunk = width // AG_CHUNKS
    n_pairs = (slots + 16) // 2 + 8
    piece = (width // 32, width)
    vertices = rows_dev * lax.axis_size("row") * lax.axis_size("col")
    bf16, f32 = jnp.bfloat16, jnp.float32
    shape = jax.ShapeDtypeStruct
    vmem = pl.BlockSpec(memory_space=pltpu.VMEM)
    smem = pl.BlockSpec(memory_space=pltpu.SMEM)
    anywhere = pl.BlockSpec(memory_space=pl.ANY)
    dma = pltpu.SemaphoreType.DMA
    limit = 56 * 1024 * 1024
    panel, feat_all, bias_rows, meta = pl.pallas_call(
        gather_body,
        out_shape=(
            shape((AG_CHUNKS, 64, ag_chunk, BLOCK), bf16),
            shape((4, width, rows_dev), bf16),
            shape((1, width), f32),
            shape((8, 384), jnp.int32),
        ),
        in_specs=[vmem] * 5 + [smem],
        out_specs=(anywhere, anywhere, vmem, vmem),
        scratch_shapes=[
            pltpu.VMEM((AG_CHUNKS, 2, ag_chunk, BLOCK), bf16),
            pltpu.VMEM((width, rows_dev), bf16),
            dma((AG_CHUNKS,)), dma((AG_CHUNKS, 64)), dma((AG_CHUNKS,)), dma((2,)), dma((1,)),
        ],
        compiler_params=pltpu.CompilerParams(
            collective_id=0, has_side_effects=True, vmem_limit_bytes=limit
        ),
    )(
        pre_act, out_grad, features,
        tile_rows.reshape(1, slots), tile_cols.reshape(1, slots), tile_counts.reshape(1, 1),
    )
    out_block = pl.BlockSpec((4, ag_chunk, rows_dev), lambda k, meta: (0, k, 0))
    own, send = pl.pallas_call(
        product_body,
        out_shape=(shape((4, width, rows_dev), f32), shape((4, width, rows_dev), bf16)),
        grid_spec=pltpu.PrefetchScalarGridSpec(
            num_scalar_prefetch=1,
            grid=(AG_CHUNKS,),
            in_specs=[
                pl.BlockSpec((None, 64, ag_chunk, BLOCK), lambda k, meta: (k, 0, 0, 0)),
                pl.BlockSpec((slots, BLOCK, BLOCK), lambda k, meta: (0, 0, 0)),
            ],
            out_specs=(out_block, out_block),
            scratch_shapes=[pltpu.VMEM((n_pairs, ag_chunk, BLOCK), f32)],
        ),
        compiler_params=pltpu.CompilerParams(vmem_limit_bytes=limit),
    )(meta, panel, tile_vals.reshape(slots, BLOCK, BLOCK))
    fg, wg, bias = pl.pallas_call(
        functools.partial(reduce_body, 1.0 / math.sqrt(vertices)),
        out_shape=(
            shape((rows_dev, width), bf16),
            shape((2, 16) + piece, f32),
            shape((8, BLOCK), f32),
        ),
        in_specs=[vmem] * 5,
        out_specs=(vmem, vmem, vmem),
        scratch_shapes=[
            pltpu.VMEM((4, width, rows_dev), bf16),
            pltpu.VMEM((width, rows_dev), f32),
            pltpu.VMEM((4, width, rows_dev), bf16),
            pltpu.VMEM((3, width, rows_dev), bf16),
            pltpu.VMEM((16,) + piece, f32),
            pltpu.VMEM((16,) + piece, f32),
            pltpu.VMEM((16,) + piece, f32),
            pltpu.VMEM((15,) + piece, f32),
            pltpu.VMEM((8,) + piece, bf16),
            pltpu.VMEM((16, 8, BLOCK), f32),
            pltpu.VMEM((8, 8, BLOCK), f32),
            pltpu.VMEM((2, 8, BLOCK), f32),
            dma((4,)), dma((4,)), dma((3,)), dma((3,)), dma((5,)), dma((5,)), dma((3,)), dma((3,)),
        ],
        compiler_params=pltpu.CompilerParams(
            collective_id=1, has_side_effects=True, vmem_limit_bytes=limit
        ),
    )(own, send, feat_all, weight, bias_rows)
    return pl.pallas_call(
        finish_body,
        out_shape=(shape((rows_dev, width), bf16), shape((width, width), f32), shape((width,), f32)),
        in_specs=[vmem] * 3,
        out_specs=(vmem, vmem, vmem),
    )(fg, wg.reshape(width, width), bias)


def solution(mesh):
    placed = (
        P(("row", "col"), None),
        P(("row", "col"), None),
        P(("row", "col"), None),
        P(),
        P("row", "col", None),
        P("row", "col", None),
        P("row", "col", None, None, None),
        P("row", "col"),
    )
    return jax.shard_map(
        local,
        mesh=mesh,
        in_specs=placed,
        out_specs=(P(("row", "col"), None), P(), P()),
        check_vma=False,
    )
```

```python
import functools
import math

import jax
import jax.numpy as jnp
from jax import lax
from jax.experimental import pallas as pl
from jax.experimental.pallas import tpu as pltpu
from jax.sharding import PartitionSpec as P

CHUNKS = 2
BLOCK = 128
MESH = pl.DeviceIdType.MESH


def body(
    norm_scale,
    pre, cot, feat, weight, trow, tcol, count, vals_hbm,
    fg_out, gathered, bias_out,
    panel0, panel1, vals, slots, feat_all, own, send1, recv1, total, send2, recv2, fg_acc,
    ar, recv_p, xs, recv_xy, zbuf, bxy, bz, bp, meta_v, meta_s,
    local_sem, ag_send, ag_recv, f_send, f_recv, rs_send1, rs_recv1, rs_send2, rs_recv2,
    ar_send, ar_recv, b_send, b_recv,
):
    rows_dev, width = pre.shape
    chunk = width // CHUNKS
    half_chunk = chunk // 2
    half = width // 2
    n_pairs = slots.shape[0]
    n_tiles = vals_hbm.shape[0]
    n_cols = 16
    panel = (panel0, panel1)

    r = lax.axis_index("row")
    c = lax.axis_index("col")
    zl, core = r // 2, r % 2
    zh, m = c // 16, c % 16
    y, x = m // 4, m % 4
    w8 = zh * 4 + zl
    partner = (r + 1 - 2 * core, c)
    z_partner = (r, (1 - zh) * 16 + m)

    def plane_peer(d):
        return (r, zh * 16 + (m + d) % 16)

    def z_peer(d):
        q = (w8 + d) % 8
        return (2 * (q % 4) + core, (q // 4) * 16 + m)

    def z_near(d):
        return (2 * ((zl + d) % 4) + core, c)

    def neighbour(dim, d):
        if dim == 0:
            return (r, zh * 16 + y * 4 + (x + d) % 4)
        return (r, zh * 16 + ((y + d) % 4) * 4 + x)

    def remote(src, dst, send_sem, recv_sem, device):
        return pltpu.make_async_remote_copy(
            src_ref=src, dst_ref=dst, send_sem=send_sem, recv_sem=recv_sem,
            device_id=device, device_id_type=MESH,
        )

    def wait_recv(ref, send_sem, recv_sem):
        remote(ref, ref, send_sem, recv_sem, partner).wait_recv()

    def wait_send(ref, send_sem, recv_sem):
        remote(ref, ref, send_sem, recv_sem, partner).wait_send()

    tiles_copy = pltpu.make_async_copy(
        vals_hbm, vals.at[pl.ds(0, n_tiles)], local_sem.at[0]
    )
    tiles_copy.start()
    barrier = pltpu.get_barrier_semaphore()

    def greet(device):
        pl.semaphore_signal(barrier, inc=1, device_id=device, device_id_type=MESH)

    greet(partner)

    def greet_plane(d, carry):
        greet(plane_peer(d))
        return carry

    def greet_z(d, carry):
        greet(z_peer(d))
        return carry

    lax.fori_loop(1, 16, greet_plane, 0)
    lax.fori_loop(1, 8, greet_z, 0)

    def block_of(plane, d1, d2, h):
        if h == 0:
            xx, yy = (x + d1) % 4, (y + d2) % 4
        else:
            xx, yy = (x + d2) % 4, (y + d1) % 4
        return 2 * (plane * 16 + yy * 4 + xx) + h

    def ag_copy(k, b, device, part=None):
        ref = panel[k].at[b]
        if part is not None:
            ref = panel[k].at[b, pl.ds(part * half_chunk, half_chunk)]
        remote(ref, ref, ag_send.at[k], ag_recv.at[k, b], device).start()

    def ag_wait(k, b):
        wait_recv(panel[k].at[b], ag_send.at[k], ag_recv.at[k, b])

    def first_dim(h):
        return 0 if h == 0 else 1

    def second_dim(h):
        return 1 if h == 0 else 0

    def s0(k, plane):
        for dim in (first_dim, second_dim):
            for h in (0, 1):
                b = block_of(plane, 0, 0, h)
                for d in (1, -1):
                    ag_copy(k, b, neighbour(dim(h), d))

    def s1(k, plane):
        for d in (-1, 1):
            for h in (0, 1):
                b = block_of(plane, d, 0, h)
                ag_wait(k, b)
                ag_copy(k, b, neighbour(first_dim(h), -d), 0 if d == -1 else 1)
                for e in (1, -1):
                    ag_copy(k, b, neighbour(second_dim(h), e))

    def s2(k, plane):
        for h in (0, 1):
            b = block_of(plane, 2, 0, h)
            ag_wait(k, b)
            for e in (1, -1):
                ag_copy(k, b, neighbour(second_dim(h), e))

    def s3(k, plane):
        for d1 in (0, -1, 1, 2):
            for d in (-1, 1):
                for h in (0, 1):
                    b = block_of(plane, d1, d, h)
                    ag_wait(k, b)
                    ag_copy(k, b, neighbour(second_dim(h), -d), 0 if d == -1 else 1)

    def s4(k, plane):
        for d1 in (0, -1, 1, 2):
            for h in (0, 1):
                ag_wait(k, block_of(plane, d1, 2, h))

    def z_go(k):
        for h in (0, 1):
            b = block_of(zh, 0, 0, h)
            ag_copy(k, b, z_partner)

    def z_come(k):
        for h in (0, 1):
            ag_wait(k, block_of(1 - zh, 0, 0, h))
        s0(k, 1 - zh)

    def prepare(k):
        lanes = pl.ds(k * chunk, chunk)
        kept = jnp.where(
            pre[:, lanes].astype(jnp.float32) > 0, cot[:, lanes].astype(jnp.float32), 0.0
        )
        for h in (0, 1):
            part = kept[h * BLOCK:(h + 1) * BLOCK, :]
            panel[k][2 * c + h] = part.T.astype(jnp.bfloat16)
        return jnp.sum(kept, axis=0, keepdims=True)

    def bias_plane(d, carry):
        remote(bxy.at[m], bxy.at[m], b_send.at[0], b_recv.at[0], plane_peer(d)).start()
        return carry

    def bias_z(d, carry):
        remote(bz.at[w8], bz.at[w8], b_send.at[1], b_recv.at[1], z_peer(d)).start()
        return carry

    bias_rows = [prepare(0)]
    pl.semaphore_wait(barrier, 23)
    s0(0, zh)
    z_go(0)
    for k in range(1, CHUNKS):
        bias_rows.append(prepare(k))
        s0(k, zh)
        z_go(k)
    bias_local = jnp.concatenate(bias_rows, axis=1)
    bxy[m] = jnp.zeros(bxy.shape[1:], jnp.float32)
    for q in range(width // BLOCK):
        bxy[m, pl.ds(q, 1)] = bias_local[:, q * BLOCK:(q + 1) * BLOCK]
    lax.fori_loop(1, 16, bias_plane, 0)
    feat_all[zl] = feat[...].astype(jnp.float32).T.astype(jnp.bfloat16)

    lane = lax.broadcasted_iota(jnp.int32, (n_tiles, n_tiles), 1)
    sub = lax.broadcasted_iota(jnp.int32, (n_tiles, n_tiles), 0)
    live = count[0, 0]
    lane1 = lax.broadcasted_iota(jnp.int32, (1, n_tiles), 1)
    col_r = jnp.where(lane1 < live, tcol[...], 100)
    diag = lane == sub
    col_c = jnp.sum(jnp.where(diag, col_r, 0), axis=1, keepdims=True)
    row_c = jnp.sum(jnp.where(diag, trow[...], 0), axis=1, keepdims=True)
    rank_c = jnp.sum(
        jnp.where((col_r == col_c) & (lane < sub), 1, 0), axis=1, keepdims=True
    )
    lane_j = lax.broadcasted_iota(jnp.int32, (n_tiles, BLOCK), 1)
    n_r = jnp.sum(jnp.where(col_c == lane_j, 1, 0), axis=0, keepdims=True)
    lane_j1 = lax.broadcasted_iota(jnp.int32, (1, BLOCK), 1)
    pad_r = jnp.where(lane_j1 < n_cols, n_r + (n_r & 1), 0)
    base_c = jnp.sum(jnp.where(lane_j < col_c, pad_r, 0), axis=1, keepdims=True)
    pos_c = jnp.where(col_c < n_cols, base_c + rank_c, 100000)
    jj_lane = lax.broadcasted_iota(jnp.int32, (BLOCK, BLOCK), 1)
    jj_sub = lax.broadcasted_iota(jnp.int32, (BLOCK, BLOCK), 0)
    pad_c = jnp.sum(jnp.where(jj_lane == jj_sub, pad_r, 0), axis=1, keepdims=True)
    end_r = jnp.sum(jnp.where(jj_sub <= jj_lane, pad_c, 0), axis=0, keepdims=True)
    last_r = jnp.maximum(end_r // 2 - 1, 0)
    has_r = jnp.where(n_r > 0, 1, 0)
    meta_w = meta_v.shape[1]
    lane_p = lax.broadcasted_iota(jnp.int32, (n_tiles, meta_w), 1)
    sub_p = lax.broadcasted_iota(jnp.int32, (n_tiles, meta_w), 0)
    for i in (0, 1):
        hit = 2 * lane_p + i == pos_c
        meta_v[i:i + 1, :] = n_tiles + jnp.sum(
            jnp.where(hit, sub_p - n_tiles, 0), axis=0, keepdims=True
        )
        meta_v[5 + i:6 + i, :] = jnp.sum(jnp.where(hit, row_c, 0), axis=0, keepdims=True)
        if i == 0:
            meta_v[2:3, :] = 1 - jnp.sum(
                jnp.where(hit & (rank_c == 0), 1, 0), axis=0, keepdims=True
            )
    meta_v[3:4, 0:BLOCK] = last_r
    meta_v[4:5, 0:BLOCK] = has_r

    meta_copy = pltpu.make_async_copy(meta_v, meta_s, local_sem.at[1])
    meta_copy.start()
    vals[n_tiles] = jnp.zeros((BLOCK, BLOCK), jnp.bfloat16)
    meta_copy.wait()

    def products(k, first, last, acc):
        def pair(p, acc):
            lhs = jnp.concatenate(
                [panel[k][meta_s[5, p]], panel[k][meta_s[6, p]]], axis=1
            )
            rhs = jnp.concatenate([vals[meta_s[0, p]], vals[meta_s[1, p]]], axis=0)
            keep = meta_s[2, p].astype(jnp.float32)
            acc = acc * keep + jnp.dot(lhs, rhs, preferred_element_type=jnp.float32)
            slots[p] = acc
            return acc

        return lax.fori_loop(first, last, pair, acc, unroll=8)

    def column(j):
        return slots[meta_s[3, j]] * meta_s[4, j].astype(jnp.float32)

    turn = [(zl + d) % 4 for d in (1, 2, 3, 0)]

    def rs0(k):
        for i, q in enumerate(turn):
            for h in (0, 1):
                lanes = slice(h * BLOCK, (h + 1) * BLOCK)
                send1[k, q, :, lanes] = column(2 * (2 * q + 1 - core) + h).astype(
                    jnp.bfloat16
                )
            remote(
                send1.at[k, q], recv1.at[k, q], rs_send1.at[k, i], rs_recv1.at[k, i], partner
            ).start()
        for q in turn:
            for h in (0, 1):
                lanes = slice(h * BLOCK, (h + 1) * BLOCK)
                own[q, :, lanes] = column(2 * (2 * q + core) + h)

    def rs1(k):
        for i, q in enumerate(turn):
            wait_recv(recv1.at[k, q], rs_send1.at[k, i], rs_recv1.at[k, i])
            pair = own[q] + recv1[k, q].astype(jnp.float32)
            send2[k, q] = pair.astype(jnp.bfloat16)
            if i < 3:
                remote(
                    send2.at[k, q], recv2.at[k, i], rs_send2.at[k, i], rs_recv2.at[k, i],
                    z_near(i + 1),
                ).start()
            else:
                total[k] = pair

    def rs2(k):
        summed = total[k]
        for d in range(3):
            wait_recv(recv2.at[k, d], rs_send2.at[k, d], rs_recv2.at[k, d])
            summed = summed + recv2[k, d].astype(jnp.float32)
        fg = jnp.dot(
            weight[:, k * chunk:(k + 1) * chunk], summed.astype(jnp.bfloat16),
            preferred_element_type=jnp.float32,
        )
        if k == 0:
            fg_acc[...] = fg
        else:
            fg_out[...] = (fg_acc[...] + fg).T.astype(jnp.bfloat16)

    def term(k, which):
        rows = pl.ds(which * half, half)
        acc = None
        for q in turn:
            piece = lax.dot_general(
                feat_all[q, rows, :], send2[k, q], (((1,), (1,)), ((), ())),
                preferred_element_type=jnp.float32,
            )
            acc = piece if acc is None else acc + piece
        return acc.reshape(recv_p.shape[1:])

    def ar0(k):
        ar[k] = term(k, 1 - core)
        remote(ar.at[k], recv_p.at[k], ar_send.at[k, 0], ar_recv.at[k, 0], partner).start()
        xs[k] = term(k, core)

    def ar1(k):
        wait_recv(recv_p.at[k], ar_send.at[k, 0], ar_recv.at[k, 0])
        xs[k] = xs[k] + recv_p[k]

        def go(d, carry):
            remote(
                xs.at[k, (m + d) % 16], recv_xy.at[k, d - 1],
                ar_send.at[k, 1], ar_recv.at[k, 1], plane_peer(d),
            ).start()
            return carry

        lax.fori_loop(1, 16, go, 0)

    def ar2(k):
        wait_recv(recv_xy.at[k], ar_send.at[k, 1], ar_recv.at[k, 1])
        zbuf[k, w8] = (xs[k, m] + jnp.sum(recv_xy[k], axis=0)).astype(zbuf.dtype)

        def go(d, carry):
            ref = zbuf.at[k, w8]
            remote(ref, ref, ar_send.at[k, 2], ar_recv.at[k, 2], z_peer(d)).start()
            return carry

        lax.fori_loop(1, 8, go, 0)

    def ar3(k):
        wait_recv(zbuf.at[k, pl.ds(0, 7)], ar_send.at[k, 2], ar_recv.at[k, 2])
        grad = zbuf[k, 0].astype(jnp.float32)
        for i in range(1, 8):
            grad = grad + zbuf[k, i].astype(jnp.float32)
        gathered[k, core, m] = grad * norm_scale

        def go(d, carry):
            ref = gathered.at[k, core, m]
            remote(ref, ref, ar_send.at[k, 3], ar_recv.at[k, 3], plane_peer(d)).start()
            return carry

        lax.fori_loop(1, 16, go, 0)

    def ar4(k):
        wait_recv(gathered.at[k, 0, pl.ds(0, 15)], ar_send.at[k, 3], ar_recv.at[k, 3])
        ref = gathered.at[k, core]
        remote(ref, ref, ar_send.at[k, 4], ar_recv.at[k, 4], partner).start()

    def bias1():
        wait_recv(bxy.at[pl.ds(0, 15)], b_send.at[0], b_recv.at[0])
        plane_sum = bxy[0]
        for i in range(1, 16):
            plane_sum = plane_sum + bxy[i]
        bz[w8] = plane_sum
        lax.fori_loop(1, 8, bias_z, 0)

    def bias2():
        wait_recv(bz.at[pl.ds(0, 7)], b_send.at[1], b_recv.at[1])
        z_sum = bz[0]
        for i in range(1, 8):
            z_sum = z_sum + bz[i]
        bp[0] = z_sum
        remote(bp.at[0], bp.at[1], b_send.at[2], b_recv.at[2], partner).start()

    other = 1 - zh
    cuts = [n_pairs * i // 32 * 8 for i in range(4)] + [n_pairs]
    s1(0, zh)
    s2(0, zh)
    z_come(0)
    s3(0, zh)
    s1(0, other)
    s2(0, other)
    s1(1, zh)
    s2(1, zh)
    z_come(1)
    for d in (1, 2, 3):
        remote(
            feat_all.at[zl], feat_all.at[zl], f_send.at[0], f_recv.at[0], z_near(d)
        ).start()
    s3(0, other)
    s4(0, zh)
    s4(0, other)
    tiles_copy.wait()
    acc = jnp.zeros((chunk, BLOCK), jnp.float32)
    acc = products(0, cuts[0], cuts[2], acc)
    s3(1, zh)
    acc = products(0, cuts[2], cuts[3], acc)
    s1(1, other)
    s2(1, other)
    products(0, cuts[3], cuts[4], acc)
    rs0(0)
    s3(1, other)
    wait_recv(feat_all.at[pl.ds(0, 3)], f_send.at[0], f_recv.at[0])
    rs1(0)
    ar0(0)
    s4(1, zh)
    s4(1, other)
    ar1(0)
    acc = jnp.zeros((chunk, BLOCK), jnp.float32)
    acc = products(1, cuts[0], cuts[2], acc)
    bias1()
    ar2(0)
    products(1, cuts[2], cuts[4], acc)
    rs0(1)
    ar3(0)
    bias2()
    rs1(1)
    ar0(1)
    rs2(0)
    ar1(1)
    ar4(0)
    ar2(1)
    wait_recv(bp.at[1], b_send.at[2], b_recv.at[2])
    bias_out[...] = (bp[0] + bp[1]) * norm_scale
    ar3(1)
    rs2(1)
    ar4(1)

    for k in range(CHUNKS):
        wait_send(panel[k].at[pl.ds(0, 62)], ag_send.at[k], ag_recv.at[k, 0])
        for i in range(4):
            wait_send(send1.at[k, 0], rs_send1.at[k, i], rs_recv1.at[k, i])
        for d in range(3):
            wait_send(recv2.at[k, d], rs_send2.at[k, d], rs_recv2.at[k, d])
        wait_send(ar.at[k], ar_send.at[k, 0], ar_recv.at[k, 0])
        wait_send(recv_xy.at[k], ar_send.at[k, 1], ar_recv.at[k, 1])
        wait_send(zbuf.at[k, pl.ds(0, 7)], ar_send.at[k, 2], ar_recv.at[k, 2])
        wait_send(gathered.at[k, 0, pl.ds(0, 15)], ar_send.at[k, 3], ar_recv.at[k, 3])
    wait_send(feat_all.at[pl.ds(0, 3)], f_send.at[0], f_recv.at[0])
    wait_send(bxy.at[pl.ds(0, 15)], b_send.at[0], b_recv.at[0])
    wait_send(bz.at[pl.ds(0, 7)], b_send.at[1], b_recv.at[1])
    wait_send(bp.at[0], b_send.at[2], b_recv.at[2])
    for k in range(CHUNKS):
        wait_recv(gathered.at[k, 0], ar_send.at[k, 4], ar_recv.at[k, 4])
        wait_send(gathered.at[k, 0], ar_send.at[k, 4], ar_recv.at[k, 4])


def finish_body(fg, wg, bias, fg_out, wg_out, bias_out):
    chunk = wg.shape[2]
    fg_out[...] = fg[...]
    for k in range(CHUNKS):
        wg_out[:, k * chunk:(k + 1) * chunk] = wg[k]
    for q in range(bias_out.shape[0] // BLOCK):
        bias_out[pl.ds(q * BLOCK, BLOCK)] = bias[q]


def local(features, pre_act, out_grad, weight, tile_rows, tile_cols, tile_vals, tile_counts):
    rows_dev, width = features.shape
    slots = tile_rows.shape[2]
    chunk = width // CHUNKS
    n_pairs = (slots + 16) // 2
    piece = (width // 32, chunk)
    vertices = rows_dev * lax.axis_size("row") * lax.axis_size("col")
    bf16, f32 = jnp.bfloat16, jnp.float32
    shape = jax.ShapeDtypeStruct
    vmem = pl.BlockSpec(memory_space=pltpu.VMEM)
    smem = pl.BlockSpec(memory_space=pltpu.SMEM)
    anywhere = pl.BlockSpec(memory_space=pl.ANY)
    dma = pltpu.SemaphoreType.DMA
    fg, wg, bias = pl.pallas_call(
        functools.partial(body, 1.0 / math.sqrt(vertices)),
        out_shape=(
            shape((rows_dev, width), bf16),
            shape((CHUNKS, 2, 16) + piece, f32),
            shape((8, BLOCK), f32),
        ),
        in_specs=[vmem] * 6 + [smem, anywhere],
        out_specs=(vmem, vmem, vmem),
        scratch_shapes=[
            pltpu.VMEM((64, chunk, BLOCK), bf16),
            pltpu.VMEM((64, chunk, BLOCK), bf16),
            pltpu.VMEM((slots + 1, BLOCK, BLOCK), bf16),
            pltpu.VMEM((n_pairs, chunk, BLOCK), f32),
            pltpu.VMEM((4, width, rows_dev), bf16),
            pltpu.VMEM((4, chunk, rows_dev), f32),
            pltpu.VMEM((CHUNKS, 4, chunk, rows_dev), bf16),
            pltpu.VMEM((CHUNKS, 4, chunk, rows_dev), bf16),
            pltpu.VMEM((CHUNKS, chunk, rows_dev), f32),
            pltpu.VMEM((CHUNKS, 4, chunk, rows_dev), bf16),
            pltpu.VMEM((CHUNKS, 3, chunk, rows_dev), bf16),
            pltpu.VMEM((width, rows_dev), f32),
            pltpu.VMEM((CHUNKS, 16) + piece, f32),
            pltpu.VMEM((CHUNKS, 16) + piece, f32),
            pltpu.VMEM((CHUNKS, 16) + piece, f32),
            pltpu.VMEM((CHUNKS, 15) + piece, f32),
            pltpu.VMEM((CHUNKS, 8) + piece, bf16),
            pltpu.VMEM((16, 8, BLOCK), f32),
            pltpu.VMEM((8, 8, BLOCK), f32),
            pltpu.VMEM((2, 8, BLOCK), f32),
            pltpu.VMEM((8, 256), jnp.int32),
            pltpu.SMEM((8, 256), jnp.int32),
            dma((2,)), dma((CHUNKS,)), dma((CHUNKS, 64)), dma((1,)), dma((1,)),
            dma((CHUNKS, 4)), dma((CHUNKS, 4)), dma((CHUNKS, 3)), dma((CHUNKS, 3)),
            dma((CHUNKS, 5)), dma((CHUNKS, 5)), dma((3,)), dma((3,)),
        ],
        compiler_params=pltpu.CompilerParams(
            collective_id=0, has_side_effects=True, vmem_limit_bytes=58 * 1024 * 1024
        ),
    )(
        pre_act, out_grad, features, weight,
        tile_rows.reshape(1, slots), tile_cols.reshape(1, slots), tile_counts.reshape(1, 1),
        tile_vals.reshape(slots, BLOCK, BLOCK),
    )
    return pl.pallas_call(
        finish_body,
        out_shape=(shape((rows_dev, width), bf16), shape((width, width), f32), shape((width,), f32)),
        in_specs=[vmem] * 3,
        out_specs=(vmem, vmem, vmem),
    )(fg, wg.reshape(CHUNKS, width, chunk), bias)


def solution(mesh):
    placed = (
        P(("row", "col"), None),
        P(("row", "col"), None),
        P(("row", "col"), None),
        P(),
        P("row", "col", None),
        P("row", "col", None),
        P("row", "col", None, None, None),
        P("row", "col"),
    )
    return jax.shard_map(
        local,
        mesh=mesh,
        in_specs=placed,
        out_specs=(P(("row", "col"), None), P(), P()),
        check_vma=False,
    )
```

```python
import functools
import math

import jax
import jax.numpy as jnp
from jax import lax
from jax.experimental import pallas as pl
from jax.experimental.pallas import tpu as pltpu
from jax.sharding import PartitionSpec as P

CHUNKS = 2
BLOCK = 128
MESH = pl.DeviceIdType.MESH


def body(
    norm_scale,
    pre, cot, feat, weight, trow, tcol, count, vals_hbm,
    fg_out, gathered, bias_out,
    panel0, panel1, vals, slots, feat_all, own, send1, recv1, total, send2, recv2, fg_acc,
    ar, recv_p, mine, xs, recv_xy, zbuf, bxy, bz, bp, meta_v, meta_s,
    local_sem, ag_send, ag_recv, f_send, f_recv, rs_send1, rs_recv1, rs_send2, rs_recv2,
    ar_send, ar_recv, b_send, b_recv,
):
    rows_dev, width = pre.shape
    chunk = width // CHUNKS
    half_chunk = chunk // 2
    half = width // 2
    n_pairs = slots.shape[0]
    n_tiles = vals_hbm.shape[0]
    n_cols = 16
    panel = (panel0, panel1)

    r = lax.axis_index("row")
    c = lax.axis_index("col")
    zl, core = r // 2, r % 2
    zh, m = c // 16, c % 16
    y, x = m // 4, m % 4
    w8 = zh * 4 + zl
    partner = (r + 1 - 2 * core, c)
    z_partner = (r, (1 - zh) * 16 + m)

    def plane_peer(d):
        return (r, zh * 16 + (m + d) % 16)

    def z_peer(d):
        q = (w8 + d) % 8
        return (2 * (q % 4) + core, (q // 4) * 16 + m)

    def z_near(d):
        return (2 * ((zl + d) % 4) + core, c)

    def neighbour(dim, d):
        if dim == 0:
            return (r, zh * 16 + y * 4 + (x + d) % 4)
        return (r, zh * 16 + ((y + d) % 4) * 4 + x)

    def remote(src, dst, send_sem, recv_sem, device):
        return pltpu.make_async_remote_copy(
            src_ref=src, dst_ref=dst, send_sem=send_sem, recv_sem=recv_sem,
            device_id=device, device_id_type=MESH,
        )

    def wait_recv(ref, send_sem, recv_sem):
        remote(ref, ref, send_sem, recv_sem, partner).wait_recv()

    def wait_send(ref, send_sem, recv_sem):
        remote(ref, ref, send_sem, recv_sem, partner).wait_send()

    tiles_copy = pltpu.make_async_copy(
        vals_hbm, vals.at[pl.ds(0, n_tiles)], local_sem.at[0]
    )
    tiles_copy.start()
    barrier = pltpu.get_barrier_semaphore()

    def greet(device):
        pl.semaphore_signal(barrier, inc=1, device_id=device, device_id_type=MESH)

    greet(partner)

    def greet_plane(d, carry):
        greet(plane_peer(d))
        return carry

    def greet_z(d, carry):
        greet(z_peer(d))
        return carry

    lax.fori_loop(1, 16, greet_plane, 0)
    lax.fori_loop(1, 8, greet_z, 0)

    def block_of(plane, d1, d2, h):
        if h == 0:
            xx, yy = (x + d1) % 4, (y + d2) % 4
        else:
            xx, yy = (x + d2) % 4, (y + d1) % 4
        return 2 * (plane * 16 + yy * 4 + xx) + h

    def ag_copy(k, b, device, part=None):
        ref = panel[k].at[b]
        if part is not None:
            ref = panel[k].at[b, pl.ds(part * half_chunk, half_chunk)]
        remote(ref, ref, ag_send.at[k], ag_recv.at[k, b], device).start()

    def ag_wait(k, b):
        wait_recv(panel[k].at[b], ag_send.at[k], ag_recv.at[k, b])

    def first_dim(h):
        return 0 if h == 0 else 1

    def second_dim(h):
        return 1 if h == 0 else 0

    def s0(k, plane):
        for dim in (first_dim, second_dim):
            for h in (0, 1):
                b = block_of(plane, 0, 0, h)
                for d in (1, -1):
                    ag_copy(k, b, neighbour(dim(h), d))

    def s1(k, plane):
        for d in (-1, 1):
            for h in (0, 1):
                b = block_of(plane, d, 0, h)
                ag_wait(k, b)
                ag_copy(k, b, neighbour(first_dim(h), -d), 0 if d == -1 else 1)
                for e in (1, -1):
                    ag_copy(k, b, neighbour(second_dim(h), e))

    def s2(k, plane):
        for h in (0, 1):
            b = block_of(plane, 2, 0, h)
            ag_wait(k, b)
            for e in (1, -1):
                ag_copy(k, b, neighbour(second_dim(h), e))

    def s3(k, plane):
        for d1 in (0, -1, 1, 2):
            for d in (-1, 1):
                for h in (0, 1):
                    b = block_of(plane, d1, d, h)
                    ag_wait(k, b)
                    ag_copy(k, b, neighbour(second_dim(h), -d), 0 if d == -1 else 1)

    def s4(k, plane):
        for d1 in (0, -1, 1, 2):
            for h in (0, 1):
                ag_wait(k, block_of(plane, d1, 2, h))

    def z_go(k):
        for h in (0, 1):
            b = block_of(zh, 0, 0, h)
            ag_copy(k, b, z_partner)

    def z_come(k):
        for h in (0, 1):
            ag_wait(k, block_of(1 - zh, 0, 0, h))
        s0(k, 1 - zh)

    def prepare(k):
        lanes = pl.ds(k * chunk, chunk)
        kept = jnp.where(
            pre[:, lanes].astype(jnp.float32) > 0, cot[:, lanes].astype(jnp.float32), 0.0
        )
        for h in (0, 1):
            part = kept[h * BLOCK:(h + 1) * BLOCK, :]
            panel[k][2 * c + h] = part.T.astype(jnp.bfloat16)
        return jnp.sum(kept, axis=0, keepdims=True)

    def bias_plane(d, carry):
        remote(bxy.at[m], bxy.at[m], b_send.at[0], b_recv.at[0], plane_peer(d)).start()
        return carry

    def bias_z(d, carry):
        remote(bz.at[w8], bz.at[w8], b_send.at[1], b_recv.at[1], z_peer(d)).start()
        return carry

    bias_rows = [prepare(0)]
    pl.semaphore_wait(barrier, 23)
    s0(0, zh)
    z_go(0)
    for k in range(1, CHUNKS):
        bias_rows.append(prepare(k))
        s0(k, zh)
        z_go(k)
    bias_local = jnp.concatenate(bias_rows, axis=1)
    bxy[m] = jnp.zeros(bxy.shape[1:], jnp.float32)
    for q in range(width // BLOCK):
        bxy[m, pl.ds(q, 1)] = bias_local[:, q * BLOCK:(q + 1) * BLOCK]
    lax.fori_loop(1, 16, bias_plane, 0)
    feat_all[zl] = feat[...].astype(jnp.float32).T.astype(jnp.bfloat16)

    lane = lax.broadcasted_iota(jnp.int32, (n_tiles, n_tiles), 1)
    sub = lax.broadcasted_iota(jnp.int32, (n_tiles, n_tiles), 0)
    live = count[0, 0]
    lane1 = lax.broadcasted_iota(jnp.int32, (1, n_tiles), 1)
    col_r = jnp.where(lane1 < live, tcol[...], 100)
    diag = lane == sub
    col_c = jnp.sum(jnp.where(diag, col_r, 0), axis=1, keepdims=True)
    row_c = jnp.sum(jnp.where(diag, trow[...], 0), axis=1, keepdims=True)
    rank_c = jnp.sum(
        jnp.where((col_r == col_c) & (lane < sub), 1, 0), axis=1, keepdims=True
    )
    lane_j = lax.broadcasted_iota(jnp.int32, (n_tiles, BLOCK), 1)
    n_r = jnp.sum(jnp.where(col_c == lane_j, 1, 0), axis=0, keepdims=True)
    lane_j1 = lax.broadcasted_iota(jnp.int32, (1, BLOCK), 1)
    pad_r = jnp.where(lane_j1 < n_cols, n_r + (n_r & 1), 0)
    base_c = jnp.sum(jnp.where(lane_j < col_c, pad_r, 0), axis=1, keepdims=True)
    pos_c = jnp.where(col_c < n_cols, base_c + rank_c, 100000)
    jj_lane = lax.broadcasted_iota(jnp.int32, (BLOCK, BLOCK), 1)
    jj_sub = lax.broadcasted_iota(jnp.int32, (BLOCK, BLOCK), 0)
    pad_c = jnp.sum(jnp.where(jj_lane == jj_sub, pad_r, 0), axis=1, keepdims=True)
    end_r = jnp.sum(jnp.where(jj_sub <= jj_lane, pad_c, 0), axis=0, keepdims=True)
    last_r = jnp.maximum(end_r // 2 - 1, 0)
    has_r = jnp.where(n_r > 0, 1, 0)
    meta_w = meta_v.shape[1]
    lane_p = lax.broadcasted_iota(jnp.int32, (n_tiles, meta_w), 1)
    sub_p = lax.broadcasted_iota(jnp.int32, (n_tiles, meta_w), 0)
    for i in (0, 1):
        hit = 2 * lane_p + i == pos_c
        meta_v[i:i + 1, :] = n_tiles + jnp.sum(
            jnp.where(hit, sub_p - n_tiles, 0), axis=0, keepdims=True
        )
        meta_v[5 + i:6 + i, :] = jnp.sum(jnp.where(hit, row_c, 0), axis=0, keepdims=True)
        if i == 0:
            meta_v[2:3, :] = 1 - jnp.sum(
                jnp.where(hit & (rank_c == 0), 1, 0), axis=0, keepdims=True
            )
    meta_v[3:4, 0:BLOCK] = last_r
    meta_v[4:5, 0:BLOCK] = has_r

    meta_copy = pltpu.make_async_copy(meta_v, meta_s, local_sem.at[1])
    meta_copy.start()
    vals[n_tiles] = jnp.zeros((BLOCK, BLOCK), jnp.bfloat16)
    meta_copy.wait()

    def products(k, first, last, acc):
        def pair(p, acc):
            lhs = jnp.concatenate(
                [panel[k][meta_s[5, p]], panel[k][meta_s[6, p]]], axis=1
            )
            rhs = jnp.concatenate([vals[meta_s[0, p]], vals[meta_s[1, p]]], axis=0)
            keep = meta_s[2, p].astype(jnp.float32)
            acc = acc * keep + jnp.dot(lhs, rhs, preferred_element_type=jnp.float32)
            slots[p] = acc
            return acc

        return lax.fori_loop(first, last, pair, acc, unroll=8)

    def column(j):
        return slots[meta_s[3, j]] * meta_s[4, j].astype(jnp.float32)

    turn = [(zl + d) % 4 for d in (1, 2, 3, 0)]

    def rs0(k):
        for i, q in enumerate(turn):
            for h in (0, 1):
                lanes = slice(h * BLOCK, (h + 1) * BLOCK)
                send1[k, q, :, lanes] = column(2 * (2 * q + 1 - core) + h).astype(
                    jnp.bfloat16
                )
            remote(
                send1.at[k, q], recv1.at[k, q], rs_send1.at[k, i], rs_recv1.at[k, i], partner
            ).start()
        for q in turn:
            for h in (0, 1):
                lanes = slice(h * BLOCK, (h + 1) * BLOCK)
                own[q, :, lanes] = column(2 * (2 * q + core) + h)

    def rs1(k):
        for i, q in enumerate(turn):
            wait_recv(recv1.at[k, q], rs_send1.at[k, i], rs_recv1.at[k, i])
            pair = own[q] + recv1[k, q].astype(jnp.float32)
            send2[k, q] = pair.astype(jnp.bfloat16)
            if i < 3:
                remote(
                    send2.at[k, q], recv2.at[k, i], rs_send2.at[k, i], rs_recv2.at[k, i],
                    z_near(i + 1),
                ).start()
            else:
                total[k] = pair

    def rs2(k):
        summed = total[k]
        for d in range(3):
            wait_recv(recv2.at[k, d], rs_send2.at[k, d], rs_recv2.at[k, d])
            summed = summed + recv2[k, d].astype(jnp.float32)
        fg = jnp.dot(
            weight[:, k * chunk:(k + 1) * chunk], summed.astype(jnp.bfloat16),
            preferred_element_type=jnp.float32,
        )
        if k == 0:
            fg_acc[...] = fg
        else:
            fg_out[...] = (fg_acc[...] + fg).T.astype(jnp.bfloat16)

    def term(k, which):
        rows = pl.ds(which * half, half)
        acc = None
        for q in turn:
            piece = lax.dot_general(
                feat_all[q, rows, :], send2[k, q], (((1,), (1,)), ((), ())),
                preferred_element_type=jnp.float32,
            )
            acc = piece if acc is None else acc + piece
        return acc.reshape(recv_p.shape[1:])

    def ar0(k):
        ar[k] = term(k, 1 - core).astype(ar.dtype)
        remote(ar.at[k], recv_p.at[k], ar_send.at[k, 0], ar_recv.at[k, 0], partner).start()
        mine[k] = term(k, core)

    def ar1(k):
        wait_recv(recv_p.at[k], ar_send.at[k, 0], ar_recv.at[k, 0])
        xs[k] = (mine[k] + recv_p[k].astype(jnp.float32)).astype(xs.dtype)

        def go(d, carry):
            remote(
                xs.at[k, (m + d) % 16], recv_xy.at[k, d - 1],
                ar_send.at[k, 1], ar_recv.at[k, 1], plane_peer(d),
            ).start()
            return carry

        lax.fori_loop(1, 16, go, 0)

    def ar2(k):
        wait_recv(recv_xy.at[k], ar_send.at[k, 1], ar_recv.at[k, 1])
        plane_sum = xs[k, m].astype(jnp.float32)
        for i in range(15):
            plane_sum = plane_sum + recv_xy[k, i].astype(jnp.float32)
        zbuf[k, w8] = plane_sum.astype(zbuf.dtype)

        def go(d, carry):
            ref = zbuf.at[k, w8]
            remote(ref, ref, ar_send.at[k, 2], ar_recv.at[k, 2], z_peer(d)).start()
            return carry

        lax.fori_loop(1, 8, go, 0)

    def ar3(k):
        wait_recv(zbuf.at[k, pl.ds(0, 7)], ar_send.at[k, 2], ar_recv.at[k, 2])
        grad = zbuf[k, 0].astype(jnp.float32)
        for i in range(1, 8):
            grad = grad + zbuf[k, i].astype(jnp.float32)
        gathered[k, core, m] = (grad * norm_scale).astype(gathered.dtype)

        def go(d, carry):
            ref = gathered.at[k, core, m]
            remote(ref, ref, ar_send.at[k, 3], ar_recv.at[k, 3], plane_peer(d)).start()
            return carry

        lax.fori_loop(1, 16, go, 0)

    def ar4(k):
        wait_recv(gathered.at[k, 0, pl.ds(0, 15)], ar_send.at[k, 3], ar_recv.at[k, 3])
        ref = gathered.at[k, core]
        remote(ref, ref, ar_send.at[k, 4], ar_recv.at[k, 4], partner).start()

    def bias1():
        wait_recv(bxy.at[pl.ds(0, 15)], b_send.at[0], b_recv.at[0])
        plane_sum = bxy[0]
        for i in range(1, 16):
            plane_sum = plane_sum + bxy[i]
        bz[w8] = plane_sum
        lax.fori_loop(1, 8, bias_z, 0)

    def bias2():
        wait_recv(bz.at[pl.ds(0, 7)], b_send.at[1], b_recv.at[1])
        z_sum = bz[0]
        for i in range(1, 8):
            z_sum = z_sum + bz[i]
        bp[0] = z_sum
        remote(bp.at[0], bp.at[1], b_send.at[2], b_recv.at[2], partner).start()

    other = 1 - zh
    cuts = [n_pairs * i // 32 * 8 for i in range(4)] + [n_pairs]
    s1(0, zh)
    s2(0, zh)
    z_come(0)
    s3(0, zh)
    s1(0, other)
    s2(0, other)
    s1(1, zh)
    s2(1, zh)
    z_come(1)
    for d in (1, 2, 3):
        remote(
            feat_all.at[zl], feat_all.at[zl], f_send.at[0], f_recv.at[0], z_near(d)
        ).start()
    s3(0, other)
    s4(0, zh)
    s4(0, other)
    tiles_copy.wait()
    acc = jnp.zeros((chunk, BLOCK), jnp.float32)
    acc = products(0, cuts[0], cuts[2], acc)
    s3(1, zh)
    acc = products(0, cuts[2], cuts[3], acc)
    s1(1, other)
    s2(1, other)
    products(0, cuts[3], cuts[4], acc)
    rs0(0)
    s3(1, other)
    wait_recv(feat_all.at[pl.ds(0, 3)], f_send.at[0], f_recv.at[0])
    rs1(0)
    ar0(0)
    s4(1, zh)
    s4(1, other)
    acc = jnp.zeros((chunk, BLOCK), jnp.float32)
    products(1, cuts[0], cuts[4], acc)
    rs0(1)
    ar1(0)
    bias1()
    rs1(1)
    ar0(1)
    rs2(0)
    ar1(1)
    bias2()
    ar2(0)
    ar2(1)
    wait_recv(bp.at[1], b_send.at[2], b_recv.at[2])
    bias_out[...] = (bp[0] + bp[1]) * norm_scale
    ar3(0)
    ar3(1)
    rs2(1)
    ar4(0)
    ar4(1)

    for k in range(CHUNKS):
        wait_send(panel[k].at[pl.ds(0, 62)], ag_send.at[k], ag_recv.at[k, 0])
        for i in range(4):
            wait_send(send1.at[k, 0], rs_send1.at[k, i], rs_recv1.at[k, i])
        for d in range(3):
            wait_send(recv2.at[k, d], rs_send2.at[k, d], rs_recv2.at[k, d])
        wait_send(ar.at[k], ar_send.at[k, 0], ar_recv.at[k, 0])
        wait_send(recv_xy.at[k], ar_send.at[k, 1], ar_recv.at[k, 1])
        wait_send(zbuf.at[k, pl.ds(0, 7)], ar_send.at[k, 2], ar_recv.at[k, 2])
        wait_send(gathered.at[k, 0, pl.ds(0, 15)], ar_send.at[k, 3], ar_recv.at[k, 3])
    wait_send(feat_all.at[pl.ds(0, 3)], f_send.at[0], f_recv.at[0])
    wait_send(bxy.at[pl.ds(0, 15)], b_send.at[0], b_recv.at[0])
    wait_send(bz.at[pl.ds(0, 7)], b_send.at[1], b_recv.at[1])
    wait_send(bp.at[0], b_send.at[2], b_recv.at[2])
    for k in range(CHUNKS):
        wait_recv(gathered.at[k, 0], ar_send.at[k, 4], ar_recv.at[k, 4])
        wait_send(gathered.at[k, 0], ar_send.at[k, 4], ar_recv.at[k, 4])


def finish_body(fg, wg, bias, fg_out, wg_out, bias_out):
    chunk = wg.shape[2]
    fg_out[...] = fg[...]
    for k in range(CHUNKS):
        wg_out[:, k * chunk:(k + 1) * chunk] = wg[k].astype(jnp.float32)
    for q in range(bias_out.shape[0] // BLOCK):
        bias_out[pl.ds(q * BLOCK, BLOCK)] = bias[q]


def local(features, pre_act, out_grad, weight, tile_rows, tile_cols, tile_vals, tile_counts):
    rows_dev, width = features.shape
    slots = tile_rows.shape[2]
    chunk = width // CHUNKS
    n_pairs = (slots + 16) // 2
    piece = (width // 32, chunk)
    vertices = rows_dev * lax.axis_size("row") * lax.axis_size("col")
    bf16, f32 = jnp.bfloat16, jnp.float32
    shape = jax.ShapeDtypeStruct
    vmem = pl.BlockSpec(memory_space=pltpu.VMEM)
    smem = pl.BlockSpec(memory_space=pltpu.SMEM)
    anywhere = pl.BlockSpec(memory_space=pl.ANY)
    dma = pltpu.SemaphoreType.DMA
    fg, wg, bias = pl.pallas_call(
        functools.partial(body, 1.0 / math.sqrt(vertices)),
        out_shape=(
            shape((rows_dev, width), bf16),
            shape((CHUNKS, 2, 16) + piece, bf16),
            shape((8, BLOCK), f32),
        ),
        in_specs=[vmem] * 6 + [smem, anywhere],
        out_specs=(vmem, vmem, vmem),
        scratch_shapes=[
            pltpu.VMEM((64, chunk, BLOCK), bf16),
            pltpu.VMEM((64, chunk, BLOCK), bf16),
            pltpu.VMEM((slots + 1, BLOCK, BLOCK), bf16),
            pltpu.VMEM((n_pairs, chunk, BLOCK), f32),
            pltpu.VMEM((4, width, rows_dev), bf16),
            pltpu.VMEM((4, chunk, rows_dev), f32),
            pltpu.VMEM((CHUNKS, 4, chunk, rows_dev), bf16),
            pltpu.VMEM((CHUNKS, 4, chunk, rows_dev), bf16),
            pltpu.VMEM((CHUNKS, chunk, rows_dev), f32),
            pltpu.VMEM((CHUNKS, 4, chunk, rows_dev), bf16),
            pltpu.VMEM((CHUNKS, 3, chunk, rows_dev), bf16),
            pltpu.VMEM((width, rows_dev), f32),
            pltpu.VMEM((CHUNKS, 16) + piece, bf16),
            pltpu.VMEM((CHUNKS, 16) + piece, bf16),
            pltpu.VMEM((CHUNKS, 16) + piece, f32),
            pltpu.VMEM((CHUNKS, 16) + piece, bf16),
            pltpu.VMEM((CHUNKS, 15) + piece, bf16),
            pltpu.VMEM((CHUNKS, 8) + piece, bf16),
            pltpu.VMEM((16, 8, BLOCK), f32),
            pltpu.VMEM((8, 8, BLOCK), f32),
            pltpu.VMEM((2, 8, BLOCK), f32),
            pltpu.VMEM((8, 256), jnp.int32),
            pltpu.SMEM((8, 256), jnp.int32),
            dma((2,)), dma((CHUNKS,)), dma((CHUNKS, 64)), dma((1,)), dma((1,)),
            dma((CHUNKS, 4)), dma((CHUNKS, 4)), dma((CHUNKS, 3)), dma((CHUNKS, 3)),
            dma((CHUNKS, 5)), dma((CHUNKS, 5)), dma((3,)), dma((3,)),
        ],
        compiler_params=pltpu.CompilerParams(
            collective_id=0, has_side_effects=True, vmem_limit_bytes=58 * 1024 * 1024
        ),
    )(
        pre_act, out_grad, features, weight,
        tile_rows.reshape(1, slots), tile_cols.reshape(1, slots), tile_counts.reshape(1, 1),
        tile_vals.reshape(slots, BLOCK, BLOCK),
    )
    return pl.pallas_call(
        finish_body,
        out_shape=(shape((rows_dev, width), bf16), shape((width, width), f32), shape((width,), f32)),
        in_specs=[vmem] * 3,
        out_specs=(vmem, vmem, vmem),
    )(fg, wg.reshape(CHUNKS, width, chunk), bias)


def solution(mesh):
    placed = (
        P(("row", "col"), None),
        P(("row", "col"), None),
        P(("row", "col"), None),
        P(),
        P("row", "col", None),
        P("row", "col", None),
        P("row", "col", None, None, None),
        P("row", "col"),
    )
    return jax.shard_map(
        local,
        mesh=mesh,
        in_specs=placed,
        out_specs=(P(("row", "col"), None), P(), P()),
        check_vma=False,
    )
```
